256 devices in a mesh: row: 16 (over z, core), col: 16 (over x, y).
Axes of the slice: x: 4, y: 4, z: 8, core: 2. Of those that a mesh axis runs over, the one named last changes fastest.
Arguments:
- start: float32 [2048, 1024], P(('row', 'col'))
- stiff: float32 [2048, 64, 576], P(('row', 'col'))
- convect: float32 [2048, 64, 64], P(('row', 'col')), may hold values from -0.1875 to 0.1875
- column_index: int32 [2048, 9], P(('row', 'col')), may hold values from 0 to 2047, as said below
- upwind: int32 [2048, 9], P(('row', 'col')), may hold values 0 or 1
Outputs:
- basis_first: float32 [2048, 5120], P(('row', 'col'))
- basis_second: float32 [2048, 4096], P(('row', 'col'))
- factor_first: float32 [80, 80], replicated
- coupling: float32 [80, 64], replicated
- factor_second: float32 [64, 64], replicated
The draws below stay inside these ranges and needn't reach their ends.
Inputs may be any that keep to these rules, and one draw needn't show every extreme that they name: `column_index`: slot 0 of block row b is b itself. Slots 1 to 6 lie in the block row's own sector (block rows s * 128 to (s + 1) * 128 - 1 for sector s), slot 7 in the previous sector and slot 8 in the next one, cyclically over the 16 sectors.
All inputs are finite; a program needn't handle non-finite values. No bound on the sum of `upwind` on one device may be relied on, other than what follows from the above.
Results may differ from the reference program's by a relative error of at most 0.0003.
Values sent between devices are 32-bit elements; how exact they have to be, the bound alone decides.
A program may use at most 128 MiB of HBM per device.

```python
import jax
import jax.numpy as jnp
from jax import lax

BS = 64
RHS = 16
SLOTS = 9
STEPS = 4
GROUP = 128
SECTORS = 16
BLOCKS = 2048
ROWS = 131072
PANEL = 80
NEWCOLS = 64


def draw_start(key, part):
    key = jax.random.fold_in(key, 12)
    rising = 1.0 + 2.0 * lax.broadcasted_iota(jnp.float32, (BLOCKS, 1), 0) / (BLOCKS - 1)
    values = jax.random.normal(key, (BLOCKS, RHS * BS), jnp.float32)
    return values * rising


def draw_stiff(key, part):
    key = jax.random.fold_in(key, 11)
    first_key, second_key = jax.random.split(key)
    shape = (BLOCKS, BS, SLOTS * BS)
    base = 0.03 * jax.random.normal(first_key, shape, jnp.float32)
    diagonal = jax.random.uniform(second_key, (BLOCKS, BS, 1), jnp.float32, 0.8, 1.2)
    on_diag = lax.broadcasted_iota(jnp.int32, (1, BS, SLOTS * BS), 2) == lax.broadcasted_iota(jnp.int32, (1, BS, SLOTS * BS), 1)
    return base + on_diag.astype(jnp.float32) * diagonal


def draw_column_index(key, part):
    key = jax.random.fold_in(key, 13)
    offsets = jax.random.randint(key, (BLOCKS, SLOTS), 0, GROUP, jnp.int32)
    row_ids = lax.broadcasted_iota(jnp.int32, (BLOCKS, SLOTS), 0)
    slot_ids = lax.broadcasted_iota(jnp.int32, (BLOCKS, SLOTS), 1)
    sector = row_ids // GROUP
    before = (sector + SECTORS - 1) % SECTORS
    after = (sector + 1) % SECTORS
    chosen = jnp.where(slot_ids == SLOTS - 2, before, jnp.where(slot_ids == SLOTS - 1, after, sector))
    result = chosen * GROUP + offsets
    return jnp.where(slot_ids == 0, row_ids, result).astype(jnp.int32)


def set_ends(values, stream_key, least, largest):
    extent = values.shape
    place = [jax.random.randint(jax.random.fold_in(stream_key, axis), (), 0, extent[axis]) for axis in range(len(extent))]
    values = values.at[tuple(place)].set(least)
    longest = extent.index(max(extent))
    place[longest] = (place[longest] + 1) % extent[longest]
    return values.at[tuple(place)].set(largest)


def levels(key, shape, cuts, smallest, largest):
    gain = 1.0
    for position, blocks in cuts:
        draws = jax.random.uniform(jax.random.fold_in(jax.random.fold_in(key, 6), position), (blocks,), jnp.float32, smallest / len(cuts), largest / len(cuts))
        gain = gain * jnp.repeat(jnp.exp(draws), shape[position] // blocks).reshape((-1,) + (1,) * (len(shape) - 1 - position))
    return gain


def normal_values(stream_key, shape, spread, limit, cuts=(), kind=jnp.bfloat16):
    loudness = levels(stream_key, shape, cuts, -0.22, 0.18) if cuts else 1.0
    entries = jax.random.normal(stream_key, shape, jnp.float32) * spread * loudness
    return jnp.minimum(jnp.maximum(entries, -limit), limit).astype(kind)


def setup_inputs(seed: int = 0) -> dict:
    seeds = jax.random.split(jax.random.key(seed), 6)
    return {
        "start": draw_start(jax.random.fold_in(seeds[5], 71), 0),
        "stiff": draw_stiff(jax.random.fold_in(seeds[5], 71), 0),
        "convect": normal_values(seeds[2], (BLOCKS, BS, BS), (16 * BS) ** -0.5, 0.1875, ((0, 256),), jnp.float32),
        "column_index": draw_column_index(jax.random.fold_in(seeds[5], 71), 0),
        "upwind": set_ends((jax.random.randint(seeds[4], (BLOCKS, SLOTS), 0, 2) < 1).astype(jnp.int32), jax.random.fold_in(seeds[4], 1), 0, 1),
    }


def apply_matrix(vector, stiff, convect, column_index, upwind):
    field = vector.reshape(BLOCKS, RHS, BS)
    near = field[column_index]
    weights = stiff.reshape(BLOCKS, BS, SLOTS, BS)
    result = jnp.einsum('bijk,bjrk->bri', weights, near, precision=lax.Precision.HIGHEST)
    flag_f = upwind.astype(jnp.float32)
    upwind_sum = jnp.einsum('bj,bjrk->brk', flag_f, near, precision=lax.Precision.HIGHEST)
    upwind_diff = upwind_sum - jnp.sum(flag_f, axis=1)[:, None, None] * field
    result = result + jnp.einsum('bik,brk->bri', convect, upwind_diff, precision=lax.Precision.HIGHEST)
    return result.reshape(BLOCKS, RHS * BS)

def powers(first, count, include, stiff, convect, column_index, upwind):
    current = first
    pieces = [first] if include else []
    for section in range(count):
        current = apply_matrix(current, stiff, convect, column_index, upwind)
        pieces.append(current)
    stacked = jnp.stack([piece.reshape(BLOCKS, RHS, BS) for piece in pieces], 1)
    return stacked.reshape(BLOCKS, len(pieces) * RHS, BS)

def finish(panel, lower):
    width = lower.shape[0]
    inverse = jax.scipy.linalg.solve_triangular(lower, jnp.eye(width, dtype=jnp.float32), lower=True)
    basis = jnp.einsum('pq,bqi->bpi', inverse, panel, precision=lax.Precision.HIGHEST)
    return (basis, lower.T)

def reference(start, stiff, convect, column_index, upwind):
    panel = powers(start, STEPS, True, stiff, convect, column_index, upwind)
    gram_one = jnp.einsum('bpi,bqi->pq', panel, panel, precision=lax.Precision.HIGHEST) / ROWS
    basis_one, factor_one = finish(panel, jnp.linalg.cholesky(gram_one))
    last_block = basis_one[:, STEPS * RHS:, :].reshape(BLOCKS, RHS * BS)
    fresh = powers(last_block, STEPS, False, stiff, convect, column_index, upwind)
    coupling = jnp.einsum('bpi,bqi->pq', basis_one, fresh, precision=lax.Precision.HIGHEST) / ROWS
    projected = fresh - jnp.einsum('pq,bpi->bqi', coupling, basis_one, precision=lax.Precision.HIGHEST)
    gram_two = jnp.einsum('bpi,bqi->pq', projected, projected, precision=lax.Precision.HIGHEST) / ROWS
    basis_two, factor_two = finish(projected, jnp.linalg.cholesky(gram_two))
    return (basis_one.reshape(BLOCKS, PANEL * BS), basis_two.reshape(BLOCKS, NEWCOLS * BS), factor_one, coupling, factor_two)
```

```python
import functools

import jax
import jax.numpy as jnp
from jax import lax
from jax.experimental import pallas as pl
from jax.experimental.pallas import tpu as pltpu
from jax.sharding import PartitionSpec as P

MESH = pl.DeviceIdType.MESH
HIGHEST = lax.Precision.HIGHEST
STEPS = 4
POWERS = 2 * STEPS
BS = 64
RHS = 16
SLOTS = 9
OWN = 8
COLS = 16
ROWS_AXIS = 16
GROUP = OWN * COLS
PANEL = (STEPS + 1) * RHS
NEW = STEPS * RHS
ALL = (POWERS + 1) * RHS
WIDE = OWN * BS
SCALE = 1.0 / (GROUP * ROWS_AXIS * BS)


def dot(a, b, contract):
    return lax.dot_general(
        a, b, (contract, ((), ())), precision=HIGHEST, preferred_element_type=jnp.float32
    )


def nt(a, b):
    return dot(a, b, ((1,), (1,)))


def nn(a, b):
    return dot(a, b, ((1,), (0,)))


def tn(a, b):
    return dot(a, b, ((0,), (0,)))


def local_row(index):
    return lax.rem(index, GROUP)


def side_by_side(a, b):
    low = lax.broadcasted_iota(jnp.int32, a.shape, 1) < BS
    top = jnp.where(low, a, pltpu.roll(b, BS, 1))
    bottom = jnp.where(low, pltpu.roll(a, BS, 1), b)
    return jnp.concatenate([top, bottom], 0)


def factor(gram):
    n = gram.shape[0]
    shape = (n, n)
    sub = lax.broadcasted_iota(jnp.int32, shape, 0)
    lane = lax.broadcasted_iota(jnp.int32, shape, 1)
    lane_row = lax.broadcasted_iota(jnp.int32, (1, n), 1)
    sub_col = lax.broadcasted_iota(jnp.int32, (n, 1), 0)

    def step(k, state):
        left, right = state
        here = sub == k
        row_left = jnp.sum(jnp.where(here, left, 0.0), 0, keepdims=True)
        row_right = jnp.sum(jnp.where(here, right, 0.0), 0, keepdims=True)
        column = jnp.sum(jnp.where(lane == k, left, 0.0), 1, keepdims=True)
        pivot = jnp.sum(jnp.where(lane_row == k, row_left, 0.0), 1, keepdims=True)
        gain = jnp.where(sub_col > k, column / pivot, 0.0)
        return left - gain * row_left, right - gain * row_right

    eye = jnp.where(sub == lane, 1.0, 0.0)
    left, right = lax.fori_loop(0, n, step, (gram, eye))
    pivots = jnp.sum(jnp.where(sub == lane, left, 0.0), 1, keepdims=True)
    scale = lax.rsqrt(pivots)
    scale = scale * (1.5 - 0.5 * pivots * scale * scale)
    return jnp.where(lane >= sub, left, 0.0) * scale, right * scale


def kernel(
    start_ref, stiff_ref, convect_ref, index_ref, index_vmem, upwind_ref,
    first_ref, second_ref, factor_first_ref, coupling_ref, factor_second_ref,
    field, rows_prev, rows_next, give, w_main, w_far, partial, powers, w_all,
    index_in, index_next, index_prev,
    sum_in, sum_a, sum_b, sum_out,
    send_sem, recv_sem, far_send, far_recv, index_send, index_recv, index_local,
    sum_send, sum_recv,
):
    row = lax.axis_index("row")
    col = lax.axis_index("col")
    sector_peers = [(row, lax.rem(col + i, COLS)) for i in range(1, COLS)]
    row_peers = [(lax.rem(row + i, ROWS_AXIS), col) for i in range(1, ROWS_AXIS)]
    nxt, prv = row_peers[0], row_peers[-1]

    barrier = pltpu.get_barrier_semaphore()
    for peer in sector_peers + row_peers:
        pl.semaphore_signal(barrier, inc=1, device_id=peer, device_id_type=MESH)
    own = pl.ds(col * OWN, OWN)
    field[0][own] = start_ref[...]
    pl.semaphore_wait(barrier, COLS + ROWS_AXIS - 2)

    pending = []

    def push(src, dst, send, recv, peer):
        copy = pltpu.make_async_remote_copy(
            src_ref=src, dst_ref=dst, send_sem=send, recv_sem=recv, device_id=peer, device_id_type=MESH
        )
        copy.start()
        pending.append(copy)
        return copy

    def arrived(ref, sem):
        pltpu.make_async_copy(ref, ref, sem).wait()

    def spread(t):
        mine = field[t].at[own]
        for i, peer in enumerate(sector_peers):
            push(mine, mine, send_sem.at[t, i], recv_sem.at[t, col], peer)

    def gathered(t):
        for i in range(1, COLS):
            other = lax.rem(col + i, COLS)
            arrived(field[t].at[pl.ds(other * OWN, OWN)], recv_sem.at[t, other])

    def keep(t, rows):
        for b in range(0, OWN, 2):
            powers[t * RHS : (t + 1) * RHS, b * BS : (b + 2) * BS] = rows(b)

    def sum_first(s, tiles):
        for i in range(tiles):
            @pl.when(col != i)
            def _(i=i):
                copy = pltpu.make_async_remote_copy(
                    src_ref=sum_in[s].at[i], dst_ref=sum_a[s].at[col], send_sem=sum_send.at[s, 0, i],
                    recv_sem=sum_recv.at[s, 0, col], device_id=(row, i), device_id_type=MESH,
                )
                copy.start()

    def sum_second(s, tiles):
        for i in range(tiles):
            @pl.when(col != i)
            def _(i=i):
                pltpu.make_async_copy(sum_in[s].at[i], sum_in[s].at[i], sum_send.at[s, 0, i]).wait()

        @pl.when(col < tiles)
        def _():
            sum_a[s][col] = sum_in[s][col]
            for i in range(1, COLS):
                other = lax.rem(col + i, COLS)
                arrived(sum_a[s].at[other], sum_recv.at[s, 0, other])
            total = sum_a[s][0]
            for i in range(1, COLS):
                total = total + sum_a[s][i]
            sum_b[s][row] = total
            for i, peer in enumerate(row_peers):
                pltpu.make_async_remote_copy(
                    src_ref=sum_b[s].at[row], dst_ref=sum_b[s].at[row], send_sem=sum_send.at[s, 1, i],
                    recv_sem=sum_recv.at[s, 1, row], device_id=peer, device_id_type=MESH,
                ).start()

    def sum_third(s, tiles):
        @pl.when(col < tiles)
        def _():
            for i in range(1, ROWS_AXIS):
                other = lax.rem(row + i, ROWS_AXIS)
                arrived(sum_b[s].at[other], sum_recv.at[s, 1, other])
            for i in range(ROWS_AXIS - 1):
                pltpu.make_async_copy(sum_b[s].at[row], sum_b[s].at[row], sum_send.at[s, 1, i]).wait()
            total = sum_b[s][0]
            for i in range(1, ROWS_AXIS):
                total = total + sum_b[s][i]
            sum_out[s][col] = total
            for i, peer in enumerate(sector_peers):
                pltpu.make_async_remote_copy(
                    src_ref=sum_out[s].at[col], dst_ref=sum_out[s].at[col], send_sem=sum_send.at[s, 2, i],
                    recv_sem=sum_recv.at[s, 2, col], device_id=peer, device_id_type=MESH,
                ).start()

    def sum_end(s, tiles):
        for i in range(tiles):
            @pl.when(col != i)
            def _(i=i):
                arrived(sum_out[s].at[i], sum_recv.at[s, 2, i])

        @pl.when(col < tiles)
        def _():
            for i in range(COLS - 1):
                pltpu.make_async_copy(sum_out[s].at[col], sum_out[s].at[col], sum_send.at[s, 2, i]).wait()

    spread(0)
    push(index_vmem, index_in.at[0], index_send.at[0], index_recv.at[0], nxt)
    push(index_vmem, index_in.at[1], index_send.at[1], index_recv.at[1], prv)
    keep(0, lambda b: side_by_side(start_ref[b], start_ref[b + 1]))

    zero = jnp.zeros((BS, BS), jnp.float32)
    for b in range(OWN):
        flags = [upwind_ref[b, j].astype(jnp.float32) for j in range(SLOTS)]
        total = functools.reduce(lambda x, y: x + y, flags)
        flags[0] = flags[0] - total
        convect = convect_ref[b]
        blocks = [stiff_ref[b, :, j * BS : (j + 1) * BS] + flags[j] * convect for j in range(SLOTS)]
        for j in range(0, 6, 2):
            w_main[b, :, j * BS : (j + 2) * BS] = jnp.concatenate(blocks[j : j + 2], 1)
        w_main[b, :, 6 * BS : 8 * BS] = jnp.concatenate([blocks[6], zero], 1)
        w_far[b] = jnp.concatenate(blocks[7:9], 1)

    arrived(index_in.at[0], index_recv.at[0])
    arrived(index_in.at[1], index_recv.at[1])
    local = [
        pltpu.make_async_copy(index_in.at[0], index_prev, index_local.at[0]),
        pltpu.make_async_copy(index_in.at[1], index_next, index_local.at[1]),
    ]
    for copy in local:
        copy.start()
    for copy in local:
        copy.wait()

    def apply(t):
        f = field[t]
        gathered(t)
        for b in range(OWN):
            give[t][0, b] = f[local_row(index_next[b, SLOTS - 2])]
            give[t][1, b] = f[local_row(index_prev[b, SLOTS - 1])]
        push(give[t].at[0], rows_prev[t], far_send.at[t, 0], far_recv.at[t, 0], nxt)
        push(give[t].at[1], rows_next[t], far_send.at[t, 1], far_recv.at[t, 1], prv)
        for b in range(OWN):
            tiles = [f[col * OWN + b]] + [f[local_row(index_ref[b, j])] for j in range(1, 7)]
            tiles.append(jnp.zeros_like(tiles[0]))
            near = jnp.concatenate([side_by_side(tiles[j], tiles[j + 1]) for j in range(0, 8, 2)], 1)
            partial[b] = nt(near, w_main[b])
        arrived(rows_prev[t], far_recv.at[t, 0])
        arrived(rows_next[t], far_recv.at[t, 1])
        results = []
        for b in range(OWN):
            near = side_by_side(rows_prev[t][b], rows_next[t][b])
            result = partial[b] + nt(near, w_far[b])
            results.append(result)
            if t + 1 < POWERS:
                field[t + 1][col * OWN + b] = jnp.concatenate([result[:8], result[8:]], 1)
        if t + 1 < POWERS:
            spread(t + 1)
        keep(t + 1, lambda b: jnp.concatenate([results[b], results[b + 1]], 1))

    for t in range(STEPS):
        apply(t)

    tiles_one = PANEL // 8
    panel = powers[:PANEL, :]
    gram = nt(panel, panel)
    wide = jnp.concatenate([gram, jnp.zeros((PANEL, 128 - PANEL), jnp.float32)], 1)
    for i in range(tiles_one):
        sum_in[0][i] = wide[i * 8 : (i + 1) * 8]
    sum_first(0, tiles_one)
    apply(STEPS)
    sum_second(0, tiles_one)
    apply(STEPS + 1)
    sum_third(0, tiles_one)
    apply(STEPS + 2)
    sum_end(0, tiles_one)
    gram = jnp.concatenate([sum_out[0][i] for i in range(tiles_one)], 0)[:, :PANEL] * SCALE
    upper_one, inverse_one = factor(gram)
    factor_first_ref[...] = upper_one
    first = nn(inverse_one, powers[:PANEL, :])
    first_ref[...] = first
    mix = inverse_one[PANEL - RHS :]
    for k in range(1, STEPS):
        w_all[(k - 1) * RHS : k * RHS] = nn(mix, powers[k * RHS : k * RHS + PANEL])
    apply(STEPS + 3)
    w_all[NEW - RHS :] = nn(mix, powers[STEPS * RHS :])

    fresh = w_all[...]
    first = first_ref[...]
    cross = nt(first, fresh)
    square = nt(fresh, fresh)
    both = jnp.concatenate([cross, square], 0)
    half = (PANEL + NEW) // 2
    tiles_two = half // 8
    wide = jnp.concatenate([both[:half], both[half:]], 1)
    for i in range(tiles_two):
        sum_in[1][i] = wide[i * 8 : (i + 1) * 8]
    sum_first(1, tiles_two)
    sum_second(1, tiles_two)
    sum_third(1, tiles_two)
    sum_end(1, tiles_two)
    wide = jnp.concatenate([sum_out[1][i] for i in range(tiles_two)], 0) * SCALE
    coupling = jnp.concatenate([wide[:, :NEW], wide[: PANEL - half, NEW:]], 0)
    square = wide[PANEL - half :, NEW:]
    coupling_ref[...] = coupling
    gram = square - tn(coupling, coupling)
    upper_two, inverse_two = factor(gram)
    factor_second_ref[...] = upper_two
    projected = fresh - tn(coupling, first)
    second_ref[...] = nn(inverse_two, projected)

    for copy in pending:
        copy.wait_send()


def per_device(start, stiff, convect, column_index, upwind):
    tiles = start.reshape(OWN, 2, 8, BS).transpose(0, 2, 1, 3).reshape(OWN, 8, 2 * BS)
    vmem = pl.BlockSpec(memory_space=pltpu.VMEM)
    smem = pl.BlockSpec(memory_space=pltpu.SMEM)
    f32 = jnp.float32
    rows = pltpu.VMEM((OWN, 8, 128), f32)
    sums = lambda: [pltpu.VMEM((16, 8, 128), f32) for _ in range(2)]
    first, second, factor_first, coupling, factor_second = pl.pallas_call(
        kernel,
        out_shape=(
            jax.ShapeDtypeStruct((PANEL, WIDE), f32),
            jax.ShapeDtypeStruct((NEW, WIDE), f32),
            jax.ShapeDtypeStruct((PANEL, PANEL), f32),
            jax.ShapeDtypeStruct((PANEL, NEW), f32),
            jax.ShapeDtypeStruct((NEW, NEW), f32),
        ),
        in_specs=[vmem, vmem, vmem, smem, vmem, smem],
        out_specs=(vmem,) * 5,
        scratch_shapes=[
            [pltpu.VMEM((GROUP, 8, 128), f32) for _ in range(POWERS)],
            [rows for _ in range(POWERS)],
            [rows for _ in range(POWERS)],
            [pltpu.VMEM((2, OWN, 8, 128), f32) for _ in range(POWERS)],
            pltpu.VMEM((OWN, BS, 8 * BS), f32),
            pltpu.VMEM((OWN, BS, 2 * BS), f32),
            pltpu.VMEM((OWN, RHS, BS), f32),
            pltpu.VMEM((ALL, WIDE), f32),
            pltpu.VMEM((NEW, WIDE), f32),
            pltpu.VMEM((2, OWN, SLOTS), jnp.int32),
            pltpu.SMEM((OWN, SLOTS), jnp.int32),
            pltpu.SMEM((OWN, SLOTS), jnp.int32),
            sums(),
            sums(),
            sums(),
            sums(),
            pltpu.SemaphoreType.DMA((POWERS, COLS)),
            pltpu.SemaphoreType.DMA((POWERS, COLS)),
            pltpu.SemaphoreType.DMA((POWERS, 2)),
            pltpu.SemaphoreType.DMA((POWERS, 2)),
            pltpu.SemaphoreType.DMA((2,)),
            pltpu.SemaphoreType.DMA((2,)),
            pltpu.SemaphoreType.DMA((2,)),
            pltpu.SemaphoreType.DMA((2, 3, 16)),
            pltpu.SemaphoreType.DMA((2, 3, 16)),
        ],
        compiler_params=pltpu.CompilerParams(
            collective_id=0, has_side_effects=True, vmem_limit_bytes=40 << 20
        ),
    )(tiles, stiff, convect, column_index, column_index, upwind)
    blocks = lambda basis: basis.reshape(-1, OWN, BS).transpose(1, 0, 2).reshape(OWN, -1)
    return blocks(first), blocks(second), factor_first, coupling, factor_second


def solution(mesh):
    return jax.shard_map(
        per_device,
        mesh=mesh,
        in_specs=(
            P(("row", "col"), None),
            P(("row", "col"), None, None),
            P(("row", "col"), None, None),
            P(("row", "col"), None),
            P(("row", "col"), None),
        ),
        out_specs=(P(("row", "col"), None), P(("row", "col"), None), P(), P(), P()),
        check_vma=False,
    )
```

```python
import functools

import jax
import jax.numpy as jnp
from jax import lax
from jax.experimental import pallas as pl
from jax.experimental.pallas import tpu as pltpu
from jax.sharding import PartitionSpec as P

MESH = pl.DeviceIdType.MESH
HIGHEST = lax.Precision.HIGHEST
STEPS = 4
POWERS = 2 * STEPS
BS = 64
RHS = 16
SLOTS = 9
OWN = 8
COLS = 16
SIDE = 4
ROWS_AXIS = 16
GROUP = OWN * COLS
PANEL = (STEPS + 1) * RHS
NEW = STEPS * RHS
ALL = (POWERS + 1) * RHS
WIDE = OWN * BS
HALVES = 2
PART = RHS // HALVES
SCALE = 1.0 / (GROUP * ROWS_AXIS * BS)


def dot(a, b, contract):
    return lax.dot_general(
        a, b, (contract, ((), ())), precision=HIGHEST, preferred_element_type=jnp.float32
    )


def nt(a, b):
    return dot(a, b, ((1,), (1,)))


def nn(a, b):
    return dot(a, b, ((1,), (0,)))


def tn(a, b):
    return dot(a, b, ((0,), (0,)))


def local_row(index):
    return lax.rem(index, GROUP)


def side_by_side(a, b):
    low = lax.broadcasted_iota(jnp.int32, a.shape, 1) < BS
    top = jnp.where(low, a, pltpu.roll(b, BS, 1))
    bottom = jnp.where(low, pltpu.roll(a, BS, 1), b)
    return jnp.concatenate([top, bottom], 0)


def factor(gram):
    n = gram.shape[0]
    tiles = n // 8
    shape = (8, n)
    sub = lax.broadcasted_iota(jnp.int32, shape, 0)
    lane = lax.broadcasted_iota(jnp.int32, shape, 1)
    left = [gram[8 * i : 8 * i + 8] for i in range(tiles)]
    right = [jnp.where(lane == sub + 8 * i, 1.0, 0.0) for i in range(tiles)]
    upper, inverse = [], []
    for k in range(tiles):
        columns = [
            [jnp.broadcast_to(left[i][:, 8 * k + j : 8 * k + j + 1], shape) if i >= k else None for i in range(tiles)]
            for j in range(8)
        ]
        pivots = jnp.ones(shape, jnp.float32)
        for j in range(8):
            pivot = columns[j][k][j : j + 1]
            scale = 1.0 / pivot
            pivots = jnp.where(sub == j, pivot, pivots)
            across = [columns[c][k][j : j + 1] for c in range(8)]
            row_left, row_right = left[k][j : j + 1], right[k][j : j + 1]
            for i in range(k, tiles):
                gain = columns[j][i] * scale
                if i == k:
                    gain = jnp.where(sub > j, gain, 0.0)
                for c in range(j + 1, 8):
                    columns[c][i] = columns[c][i] - gain * across[c]
                left[i] = left[i] - gain * row_left
                right[i] = right[i] - gain * row_right
        scale = lax.rsqrt(pivots)
        scale = scale * (1.5 - 0.5 * pivots * scale * scale)
        upper.append(jnp.where(lane >= sub + 8 * k, left[k], 0.0) * scale)
        inverse.append(right[k] * scale)
    return jnp.concatenate(upper, 0), jnp.concatenate(inverse, 0)


def kernel(
    start_ref, stiff_hbm, convect_hbm, index_hbm, upwind_hbm,
    first_ref, second_ref, factor_first_ref, coupling_ref, factor_second_ref,
    field, rows_prev, rows_next, give, stiff_ref, convect_ref, w_main, w_far, partial, powers, w_all, mix_ref,
    index_in, index_ref, upwind_ref, index_next, index_prev,
    sum_in, sum_a, sum_b, sum_out,
    send_sem, recv_sem, far_send, far_recv, index_send, index_recv, local_sem,
    sum_send, sum_recv,
):
    row = lax.axis_index("row")
    col = lax.axis_index("col")
    away = lambda i: min(i, SIDE - i)
    steps = sorted(
        ((i, j) for i in range(SIDE) for j in range(SIDE) if i or j), key=lambda p: -away(p[0]) - away(p[1])
    )
    sector_peers = [
        (row, lax.rem(col // SIDE + i, SIDE) * SIDE + lax.rem(lax.rem(col, SIDE) + j, SIDE)) for i, j in steps
    ]
    row_peers = [(lax.rem(row + i, ROWS_AXIS), col) for i in range(1, ROWS_AXIS)]
    nxt, prv = row_peers[0], row_peers[-1]

    barrier = pltpu.get_barrier_semaphore()
    for peer in sector_peers + row_peers:
        pl.semaphore_signal(barrier, inc=1, device_id=peer, device_id_type=MESH)
    loads = [
        pltpu.make_async_copy(src, dst, local_sem.at[i])
        for i, (src, dst) in enumerate(
            [(index_hbm, index_ref), (upwind_hbm, upwind_ref), (convect_hbm, convect_ref), (stiff_hbm, stiff_ref)]
        )
    ]
    for copy in loads:
        copy.start()
    own = pl.ds(col * OWN, OWN)
    for h in range(HALVES):
        field[0][h][own] = start_ref[h]
    pl.semaphore_wait(barrier, COLS + ROWS_AXIS - 2)

    pending = []

    def push(src, dst, send, recv, peer):
        copy = pltpu.make_async_remote_copy(
            src_ref=src, dst_ref=dst, send_sem=send, recv_sem=recv, device_id=peer, device_id_type=MESH
        )
        copy.start()
        return copy

    def arrived(ref, sem):
        pltpu.make_async_copy(ref, ref, sem).wait()

    def others(t, h):
        return field[t][h].at[pl.ds(0, GROUP - OWN)]

    def spread(t, h):
        mine = field[t][h].at[own]
        for peer in sector_peers:
            push(mine, mine, send_sem.at[t, h], recv_sem.at[t, h], peer)

    def keep(t, h, rows):
        for b in range(0, OWN, 2):
            powers[t * RHS + h * PART : t * RHS + (h + 1) * PART, b * BS : (b + 2) * BS] = rows(b)

    def sum_first(s, tiles):
        for i in range(tiles):
            @pl.when(col != i)
            def _(i=i):
                copy = pltpu.make_async_remote_copy(
                    src_ref=sum_in[s].at[i], dst_ref=sum_a[s].at[col], send_sem=sum_send.at[s, 0, i],
                    recv_sem=sum_recv.at[s, 0, col], device_id=(row, i), device_id_type=MESH,
                )
                copy.start()

    def sum_second(s, tiles):
        for i in range(tiles):
            @pl.when(col != i)
            def _(i=i):
                pltpu.make_async_copy(sum_in[s].at[i], sum_in[s].at[i], sum_send.at[s, 0, i]).wait()

        @pl.when(col < tiles)
        def _():
            sum_a[s][col] = sum_in[s][col]
            for i in range(1, COLS):
                other = lax.rem(col + i, COLS)
                arrived(sum_a[s].at[other], sum_recv.at[s, 0, other])
            total = sum_a[s][0]
            for i in range(1, COLS):
                total = total + sum_a[s][i]
            sum_b[s][row] = total
            for i, peer in enumerate(row_peers):
                pltpu.make_async_remote_copy(
                    src_ref=sum_b[s].at[row], dst_ref=sum_b[s].at[row], send_sem=sum_send.at[s, 1, i],
                    recv_sem=sum_recv.at[s, 1, row], device_id=peer, device_id_type=MESH,
                ).start()

    def sum_third(s, tiles):
        @pl.when(col < tiles)
        def _():
            for i in range(1, ROWS_AXIS):
                other = lax.rem(row + i, ROWS_AXIS)
                arrived(sum_b[s].at[other], sum_recv.at[s, 1, other])
            for i in range(ROWS_AXIS - 1):
                pltpu.make_async_copy(sum_b[s].at[row], sum_b[s].at[row], sum_send.at[s, 1, i]).wait()
            total = sum_b[s][0]
            for i in range(1, ROWS_AXIS):
                total = total + sum_b[s][i]
            sum_out[s][col] = total
            for i, peer in enumerate(sector_peers):
                pltpu.make_async_remote_copy(
                    src_ref=sum_out[s].at[col], dst_ref=sum_out[s].at[col], send_sem=sum_send.at[s, 2, i],
                    recv_sem=sum_recv.at[s, 2, col], device_id=peer, device_id_type=MESH,
                ).start()

    def sum_end(s, tiles):
        for i in range(tiles):
            @pl.when(col != i)
            def _(i=i):
                arrived(sum_out[s].at[i], sum_recv.at[s, 2, i])

        @pl.when(col < tiles)
        def _():
            for i in range(COLS - 1):
                pltpu.make_async_copy(sum_out[s].at[col], sum_out[s].at[col], sum_send.at[s, 2, i]).wait()

    for h in range(HALVES):
        spread(0, h)
    pending.append(push(index_hbm, index_in.at[0], index_send.at[0], index_recv.at[0], nxt))
    pending.append(push(index_hbm, index_in.at[1], index_send.at[1], index_recv.at[1], prv))
    for h in range(HALVES):
        keep(0, h, lambda b: side_by_side(start_ref[h, b], start_ref[h, b + 1]))

    for copy in loads:
        copy.wait()
    zero = jnp.zeros((BS, BS), jnp.float32)
    for b in range(OWN):
        flags = [upwind_ref[b, j].astype(jnp.float32) for j in range(SLOTS)]
        total = functools.reduce(lambda x, y: x + y, flags)
        flags[0] = flags[0] - total
        convect = convect_ref[b]
        blocks = [stiff_ref[b, :, j * BS : (j + 1) * BS] + flags[j] * convect for j in range(SLOTS)]
        for j in range(0, 6, 2):
            w_main[b, :, j * BS : (j + 2) * BS] = jnp.concatenate(blocks[j : j + 2], 1)
        w_main[b, :, 6 * BS : 8 * BS] = jnp.concatenate([blocks[6], zero], 1)
        w_far[b] = jnp.concatenate(blocks[7:9], 1)

    arrived(index_in.at[0], index_recv.at[0])
    arrived(index_in.at[1], index_recv.at[1])
    local = [
        pltpu.make_async_copy(index_in.at[0], index_prev, local_sem.at[4]),
        pltpu.make_async_copy(index_in.at[1], index_next, local_sem.at[5]),
    ]
    for copy in local:
        copy.start()
    for copy in local:
        copy.wait()

    def apply(t, h, beside=()):
        f = field[t][h]
        arrived(others(t, h), recv_sem.at[t, h])
        for b in range(OWN):
            give[t][h][0, b] = f[local_row(index_next[b, SLOTS - 2])]
            give[t][h][1, b] = f[local_row(index_prev[b, SLOTS - 1])]
        pending.append(push(give[t][h].at[0], rows_prev[t].at[h], far_send.at[t, h, 0], far_recv.at[t, h, 0], nxt))
        pending.append(push(give[t][h].at[1], rows_next[t].at[h], far_send.at[t, h, 1], far_recv.at[t, h, 1], prv))
        for b in range(OWN):
            tiles = [f[col * OWN + b]] + [f[local_row(index_ref[b, j])] for j in range(1, 7)]
            tiles.append(jnp.zeros_like(tiles[0]))
            near = jnp.concatenate([side_by_side(tiles[j], tiles[j + 1]) for j in range(0, 8, 2)], 1)
            partial[b] = nt(near, w_main[b])
        for call in beside:
            call()
        arrived(rows_prev[t].at[h], far_recv.at[t, h, 0])
        arrived(rows_next[t].at[h], far_recv.at[t, h, 1])
        results = []
        for b in range(OWN):
            near = side_by_side(rows_prev[t][h, b], rows_next[t][h, b])
            result = partial[b] + nt(near, w_far[b])
            results.append(result)
            if t + 1 < POWERS:
                field[t + 1][h][col * OWN + b] = jnp.concatenate([result[:4], result[4:]], 1)
        if t + 1 < POWERS:
            spread(t + 1, h)
        keep(t + 1, h, lambda b: jnp.concatenate([results[b], results[b + 1]], 1))

    def gram_first():
        panel = powers[:PANEL, :]
        gram = nt(panel, panel)
        wide = jnp.concatenate([gram, jnp.zeros((PANEL, 128 - PANEL), jnp.float32)], 1)
        for i in range(tiles_one):
            sum_in[0][i] = wide[i * 8 : (i + 1) * 8]
        sum_first(0, tiles_one)

    def factor_one():
        sum_end(0, tiles_one)
        gram = jnp.concatenate([sum_out[0][i] for i in range(tiles_one)], 0)[:, :PANEL] * SCALE
        upper_one, inverse_one = factor(gram)
        factor_first_ref[...] = upper_one
        first_ref[...] = nn(inverse_one, powers[:PANEL, :])
        mix_ref[...] = inverse_one[PANEL - RHS :]

    def mix_early():
        for k in range(1, STEPS):
            w_all[(k - 1) * RHS : k * RHS] = nn(mix_ref[...], powers[k * RHS : k * RHS + PANEL])

    tiles_one = PANEL // 8
    for t in range(STEPS):
        for h in range(HALVES):
            apply(t, h)
    apply(4, 0, [gram_first])
    apply(4, 1, [lambda: sum_second(0, tiles_one)])
    apply(5, 0, [lambda: sum_third(0, tiles_one)])
    apply(5, 1)
    apply(6, 0, [factor_one])
    apply(6, 1)
    apply(7, 0, [mix_early])
    apply(7, 1)
    w_all[NEW - RHS :] = nn(mix_ref[...], powers[STEPS * RHS :])

    fresh = w_all[...]
    first = first_ref[...]
    cross = nt(first, fresh)
    square = nt(fresh, fresh)
    both = jnp.concatenate([cross, square], 0)
    half = (PANEL + NEW) // 2
    tiles_two = half // 8
    wide = jnp.concatenate([both[:half], both[half:]], 1)
    for i in range(tiles_two):
        sum_in[1][i] = wide[i * 8 : (i + 1) * 8]
    sum_first(1, tiles_two)
    sum_second(1, tiles_two)
    sum_third(1, tiles_two)
    sum_end(1, tiles_two)
    wide = jnp.concatenate([sum_out[1][i] for i in range(tiles_two)], 0) * SCALE
    coupling = jnp.concatenate([wide[:, :NEW], wide[: PANEL - half, NEW:]], 0)
    square = wide[PANEL - half :, NEW:]
    coupling_ref[...] = coupling
    gram = square - tn(coupling, coupling)
    upper_two, inverse_two = factor(gram)
    factor_second_ref[...] = upper_two
    projected = fresh - tn(coupling, first)
    second_ref[...] = nn(inverse_two, projected)

    for copy in pending:
        copy.wait_send()
    for t in range(POWERS):
        for h in range(HALVES):
            arrived(others(t, h), send_sem.at[t, h])


def per_device(start, stiff, convect, column_index, upwind):
    tiles = start.reshape(OWN, HALVES, 2, 4, BS).transpose(1, 0, 3, 2, 4).reshape(HALVES, OWN, 4, 2 * BS)
    vmem = pl.BlockSpec(memory_space=pltpu.VMEM)
    hbm = pl.BlockSpec(memory_space=pl.ANY)
    f32 = jnp.float32
    rows = pltpu.VMEM((HALVES, OWN, 4, 128), f32)
    sums = lambda: [pltpu.VMEM((16, 8, 128), f32) for _ in range(2)]
    first, second, factor_first, coupling, factor_second = pl.pallas_call(
        kernel,
        out_shape=(
            jax.ShapeDtypeStruct((PANEL, WIDE), f32),
            jax.ShapeDtypeStruct((NEW, WIDE), f32),
            jax.ShapeDtypeStruct((PANEL, PANEL), f32),
            jax.ShapeDtypeStruct((PANEL, NEW), f32),
            jax.ShapeDtypeStruct((NEW, NEW), f32),
        ),
        in_specs=[vmem, hbm, hbm, hbm, hbm],
        out_specs=(vmem,) * 5,
        scratch_shapes=[
            [[pltpu.VMEM((GROUP, 4, 128), f32) for _ in range(HALVES)] for _ in range(POWERS)],
            [rows for _ in range(POWERS)],
            [rows for _ in range(POWERS)],
            [[pltpu.VMEM((2, OWN, 4, 128), f32) for _ in range(HALVES)] for _ in range(POWERS)],
            pltpu.VMEM((OWN, BS, SLOTS * BS), f32),
            pltpu.VMEM((OWN, BS, BS), f32),
            pltpu.VMEM((OWN, BS, 8 * BS), f32),
            pltpu.VMEM((OWN, BS, 2 * BS), f32),
            pltpu.VMEM((OWN, PART, BS), f32),
            pltpu.VMEM((ALL, WIDE), f32),
            pltpu.VMEM((NEW, WIDE), f32),
            pltpu.VMEM((RHS, PANEL), f32),
            pltpu.VMEM((2, OWN, SLOTS), jnp.int32),
            pltpu.SMEM((OWN, SLOTS), jnp.int32),
            pltpu.SMEM((OWN, SLOTS), jnp.int32),
            pltpu.SMEM((OWN, SLOTS), jnp.int32),
            pltpu.SMEM((OWN, SLOTS), jnp.int32),
            sums(),
            sums(),
            sums(),
            sums(),
            pltpu.SemaphoreType.DMA((POWERS, HALVES)),
            pltpu.SemaphoreType.DMA((POWERS, HALVES)),
            pltpu.SemaphoreType.DMA((POWERS, HALVES, 2)),
            pltpu.SemaphoreType.DMA((POWERS, HALVES, 2)),
            pltpu.SemaphoreType.DMA((2,)),
            pltpu.SemaphoreType.DMA((2,)),
            pltpu.SemaphoreType.DMA((6,)),
            pltpu.SemaphoreType.DMA((2, 3, 16)),
            pltpu.SemaphoreType.DMA((2, 3, 16)),
        ],
        compiler_params=pltpu.CompilerParams(
            collective_id=0, has_side_effects=True, vmem_limit_bytes=56 << 20
        ),
    )(tiles, stiff, convect, column_index, upwind)
    blocks = lambda basis: basis.reshape(-1, OWN, BS).transpose(1, 0, 2).reshape(OWN, -1)
    return blocks(first), blocks(second), factor_first, coupling, factor_second


def solution(mesh):
    return jax.shard_map(
        per_device,
        mesh=mesh,
        in_specs=(
            P(("row", "col"), None),
            P(("row", "col"), None, None),
            P(("row", "col"), None, None),
            P(("row", "col"), None),
            P(("row", "col"), None),
        ),
        out_specs=(P(("row", "col"), None), P(("row", "col"), None), P(), P(), P()),
        check_vma=False,
    )
```

```python
import functools

import jax
import jax.numpy as jnp
from jax import lax
from jax.experimental import pallas as pl
from jax.experimental.pallas import tpu as pltpu
from jax.sharding import PartitionSpec as P

MESH = pl.DeviceIdType.MESH
HIGHEST = lax.Precision.HIGHEST
STEPS = 4
POWERS = 2 * STEPS
BS = 64
RHS = 16
SLOTS = 9
OWN = 8
COLS = 16
SIDE = 4
ROWS_AXIS = 16
GROUP = OWN * COLS
PANEL = (STEPS + 1) * RHS
NEW = STEPS * RHS
ALL = (POWERS + 1) * RHS
WIDE = OWN * BS
HALVES = 2
PART = RHS // HALVES
SCALE = 1.0 / (GROUP * ROWS_AXIS * BS)


def dot(a, b, contract):
    return lax.dot_general(
        a, b, (contract, ((), ())), precision=HIGHEST, preferred_element_type=jnp.float32
    )


def nt(a, b):
    return dot(a, b, ((1,), (1,)))


def nn(a, b):
    return dot(a, b, ((1,), (0,)))


def tn(a, b):
    return dot(a, b, ((0,), (0,)))


def local_row(index):
    return lax.bitwise_and(index, GROUP - 1)


def side_by_side(a, b):
    low = lax.broadcasted_iota(jnp.int32, a.shape, 1) < BS
    top = jnp.where(low, a, pltpu.roll(b, BS, 1))
    bottom = jnp.where(low, pltpu.roll(a, BS, 1), b)
    return jnp.concatenate([top, bottom], 0)


def factor(gram):
    n = gram.shape[0]
    tiles = n // 8
    shape = (8, n)
    sub = lax.broadcasted_iota(jnp.int32, shape, 0)
    lane = lax.broadcasted_iota(jnp.int32, shape, 1)
    left = [gram[8 * i : 8 * i + 8] for i in range(tiles)]
    right = [jnp.where(lane == sub + 8 * i, 1.0, 0.0) for i in range(tiles)]
    upper, inverse = [], []
    for k in range(tiles):
        columns = [
            [jnp.broadcast_to(left[i][:, 8 * k + j : 8 * k + j + 1], shape) if i >= k else None for i in range(tiles)]
            for j in range(8)
        ]
        pivots = jnp.ones(shape, jnp.float32)
        for j in range(8):
            pivot = columns[j][k][j : j + 1]
            scale = 1.0 / pivot
            pivots = jnp.where(sub == j, pivot, pivots)
            across = [columns[c][k][j : j + 1] for c in range(8)]
            row_left, row_right = left[k][j : j + 1], right[k][j : j + 1]
            for i in range(k, tiles):
                gain = columns[j][i] * scale
                if i == k:
                    gain = jnp.where(sub > j, gain, 0.0)
                for c in range(j + 1, 8):
                    columns[c][i] = columns[c][i] - gain * across[c]
                left[i] = left[i] - gain * row_left
                right[i] = right[i] - gain * row_right
        scale = lax.rsqrt(pivots)
        scale = scale * (1.5 - 0.5 * pivots * scale * scale)
        upper.append(jnp.where(lane >= sub + 8 * k, left[k], 0.0) * scale)
        inverse.append(right[k] * scale)
    return jnp.concatenate(upper, 0), jnp.concatenate(inverse, 0)


def kernel(
    start_ref, stiff_hbm, convect_hbm, index_hbm, upwind_hbm,
    first_ref, second_ref, factor_first_ref, coupling_ref, factor_second_ref,
    field, start_tiles, rows_twin, rows_far, give, stiff_ref, convect_ref, w_main, w_far, partial, powers, basis, mix_ref, both_ref, turn_first, turn_second,
    index_in, index_ref, upwind_ref, index_twin, index_far,
    sum_in, sum_a, sum_b, sum_out,
    send_sem, recv_sem, far_send, far_recv, index_send, index_recv, local_sem,
    sum_send, sum_recv,
):
    row = lax.axis_index("row")
    col = lax.axis_index("col")
    away = lambda i: min(i, SIDE - i)
    steps = sorted(
        ((i, j) for i in range(SIDE) for j in range(SIDE) if i or j), key=lambda p: -away(p[0]) - away(p[1])
    )
    sector_peers = [
        (row, lax.rem(col // SIDE + i, SIDE) * SIDE + lax.rem(lax.rem(col, SIDE) + j, SIDE)) for i, j in steps
    ]
    ring = sorted(range(1, ROWS_AXIS), key=lambda i: -min(i, ROWS_AXIS - i))
    row_peers = [(lax.rem(row + i, ROWS_AXIS), col) for i in ring]
    odd = lax.rem(row, 2)
    twin = (row + 1 - 2 * odd, col)
    far = (lax.rem(row + ROWS_AXIS - 1 + 2 * odd, ROWS_AXIS), col)
    slot_twin, slot_far = SLOTS - 2 + odd, SLOTS - 1 - odd

    barrier = pltpu.get_barrier_semaphore()
    for peer in sector_peers + [twin, far]:
        pl.semaphore_signal(barrier, inc=1, device_id=peer, device_id_type=MESH)
    loads = [
        pltpu.make_async_copy(src, dst, local_sem.at[i])
        for i, (src, dst) in enumerate(
            [(index_hbm, index_ref), (upwind_hbm, upwind_ref), (convect_hbm, convect_ref), (stiff_hbm, stiff_ref)]
        )
    ]
    for copy in loads:
        copy.start()
    own = pl.ds(col * OWN, OWN)
    for h in range(HALVES):
        for m in range(4):
            c = (h * PART + m) * BS
            start_tiles[h, :, m, :] = jnp.concatenate([start_ref[:, c : c + BS], start_ref[:, c + 4 * BS : c + 5 * BS]], 1)
        field[0][h][own] = start_tiles[h]
    pl.semaphore_wait(barrier, COLS + 1)

    pending = []

    def push(src, dst, send, recv, peer):
        copy = pltpu.make_async_remote_copy(
            src_ref=src, dst_ref=dst, send_sem=send, recv_sem=recv, device_id=peer, device_id_type=MESH
        )
        copy.start()
        return copy

    def arrived(ref, sem):
        pltpu.make_async_copy(ref, ref, sem).wait()

    def others(t, h):
        return field[t][h].at[pl.ds(0, GROUP - OWN)]

    def spread(t, h):
        mine = field[t][h].at[own]
        for peer in sector_peers:
            push(mine, mine, send_sem.at[t, h], recv_sem.at[t, h], peer)

    def keep(t, h, rows):
        for b in range(0, OWN, 2):
            powers[t * RHS + h * PART : t * RHS + (h + 1) * PART, b * BS : (b + 2) * BS] = rows(b)

    def sum_first(s, tiles):
        for peer in sector_peers:
            @pl.when(peer[1] < tiles)
            def _(peer=peer):
                push(sum_in[s].at[peer[1]], sum_a[s].at[col], sum_send.at[s, 0], sum_recv.at[s, 0], peer)

    def sum_second(s, tiles):
        @pl.when(col < tiles)
        def _():
            sum_a[s][col] = sum_in[s][col]
            arrived(sum_a[s].at[pl.ds(0, COLS - 1)], sum_recv.at[s, 0])
            sum_b[s][row] = total_of(sum_a[s])
            for peer in row_peers:
                push(sum_b[s].at[row], sum_b[s].at[row], sum_send.at[s, 1], sum_recv.at[s, 1], peer)

    def sum_third(s, tiles):
        @pl.when(col < tiles)
        def _():
            arrived(sum_b[s].at[pl.ds(0, ROWS_AXIS - 1)], sum_recv.at[s, 1])
            sum_out[s][col] = total_of(sum_b[s])
            for peer in sector_peers:
                push(sum_out[s].at[col], sum_out[s].at[col], sum_send.at[s, 2], sum_recv.at[s, 2], peer)

    def sum_end(s, tiles):
        @pl.when(col < tiles)
        def _():
            arrived(sum_out[s].at[pl.ds(0, tiles - 1)], sum_recv.at[s, 2])

        @pl.when(col >= tiles)
        def _():
            arrived(sum_out[s].at[pl.ds(0, tiles)], sum_recv.at[s, 2])

    def sum_sent(s, tiles):
        @pl.when(col < tiles)
        def _():
            arrived(sum_in[s].at[pl.ds(0, tiles - 1)], sum_send.at[s, 0])
            arrived(sum_b[s].at[pl.ds(0, ROWS_AXIS - 1)], sum_send.at[s, 1])
            arrived(sum_out[s].at[pl.ds(0, COLS - 1)], sum_send.at[s, 2])

        @pl.when(col >= tiles)
        def _():
            arrived(sum_in[s].at[pl.ds(0, tiles)], sum_send.at[s, 0])

    def total_of(ref):
        terms = [ref[i] for i in range(16)]
        while len(terms) > 1:
            terms = [terms[i] + terms[i + 1] for i in range(0, len(terms), 2)]
        return terms[0]

    for h in range(HALVES):
        spread(0, h)
    pending.append(push(index_hbm, index_in.at[0], index_send.at[0], index_recv.at[0], twin))
    pending.append(push(index_hbm, index_in.at[1], index_send.at[1], index_recv.at[1], far))
    for h in range(HALVES):
        keep(0, h, lambda b: side_by_side(start_tiles[h, b], start_tiles[h, b + 1]))

    for copy in loads:
        copy.wait()
    for b in range(OWN):
        flags = [upwind_ref[b, j].astype(jnp.float32) for j in range(SLOTS)]
        total = functools.reduce(lambda x, y: x + y, flags)
        flags[0] = flags[0] - total
        convect = convect_ref[b]
        blocks = [stiff_ref[b, :, j * BS : (j + 1) * BS] + flags[j] * convect for j in range(SLOTS)]
        for j in range(0, 6, 2):
            w_main[b, :, j * BS : (j + 2) * BS] = jnp.concatenate(blocks[j : j + 2], 1)
        w_main[b, :, 6 * BS : 8 * BS] = jnp.concatenate([blocks[6], jnp.zeros_like(convect)], 1)
        near_far = [jnp.where(odd == 0, blocks[8], blocks[7]), jnp.where(odd == 0, blocks[7], blocks[8])]
        w_far[b] = jnp.concatenate(near_far, 1)

    arrived(index_in.at[0], index_recv.at[0])
    arrived(index_in.at[1], index_recv.at[1])
    local = [
        pltpu.make_async_copy(index_in.at[0], index_twin, local_sem.at[4]),
        pltpu.make_async_copy(index_in.at[1], index_far, local_sem.at[5]),
    ]
    for copy in local:
        copy.start()
    for copy in local:
        copy.wait()

    def apply(t, h, beside=()):
        f = field[t][h]
        arrived(others(t, h), recv_sem.at[t, h])
        for b in range(OWN):
            give[t][h][0, b] = f[local_row(index_far[b, slot_far])]
        pending.append(push(give[t][h].at[0], rows_far[t].at[h], far_send.at[t, h, 0], far_recv.at[t, h, 0], far))
        for b in range(OWN):
            give[t][h][1, b] = f[local_row(index_twin[b, slot_twin])]
        pending.append(push(give[t][h].at[1], rows_twin[t].at[h], far_send.at[t, h, 1], far_recv.at[t, h, 1], twin))
        for b in range(OWN):
            tiles = [f[col * OWN + b]] + [f[local_row(index_ref[b, j])] for j in range(1, 7)]
            tiles.append(jnp.zeros_like(tiles[0]))
            near = jnp.concatenate([side_by_side(tiles[j], tiles[j + 1]) for j in range(0, 8, 2)], 1)
            partial[b] = nt(near, w_main[b])
        arrived(rows_twin[t].at[h], far_recv.at[t, h, 1])
        for call in beside:
            call()
        arrived(rows_far[t].at[h], far_recv.at[t, h, 0])
        results = []
        for b in range(OWN):
            result = partial[b] + nt(side_by_side(rows_twin[t][h, b], rows_far[t][h, b]), w_far[b])
            results.append(result)
            if t + 1 < POWERS:
                field[t + 1][h][col * OWN + b] = jnp.concatenate([result[:4], result[4:]], 1)
        if t + 1 < POWERS:
            spread(t + 1, h)
        keep(t + 1, h, lambda b: jnp.concatenate([results[b], results[b + 1]], 1))
        arrived(others(t, h), send_sem.at[t, h])
        for copy in pending:
            copy.wait_send()
        pending.clear()

    def gram_first():
        panel = powers[:PANEL, :]
        gram = nt(panel, panel)
        wide = jnp.concatenate([gram, jnp.zeros((PANEL, 128 - PANEL), jnp.float32)], 1)
        for i in range(tiles_one):
            sum_in[0][i] = wide[i * 8 : (i + 1) * 8]
        sum_first(0, tiles_one)

    def factor_one():
        sum_end(0, tiles_one)
        gram = jnp.concatenate([sum_out[0][i] for i in range(tiles_one)], 0)[:, :PANEL] * SCALE
        upper_one, inverse_one = factor(gram)
        factor_first_ref[...] = upper_one
        basis[:PANEL] = nn(inverse_one, powers[:PANEL, :])
        mix_ref[...] = inverse_one[PANEL - RHS :]

    def mix_early():
        for k in range(1, STEPS):
            basis[PANEL + (k - 1) * RHS : PANEL + k * RHS] = nn(mix_ref[...], powers[k * RHS : k * RHS + PANEL])
        both_ref[: PANEL + early, :early] = nt(basis[: PANEL + early], basis[PANEL : PANEL + early])

    def lay_out(value, turn, out_ref):
        n = value.shape[0]
        low = lax.broadcasted_iota(jnp.int32, (OWN, 2 * BS), 1) < BS
        for b in range(OWN):
            pair = value[:, b // 2 * 2 * BS : (b // 2 + 1) * 2 * BS]
            turn[:, b, :] = pair if b % 2 == 0 else pltpu.roll(pair, BS, 1)
        for p in range(0, n, 2):
            out_ref[:, p * BS : (p + 2) * BS] = jnp.where(low, turn[p], pltpu.roll(turn[p + 1], BS, 1))

    early = NEW - RHS
    tiles_one = PANEL // 8
    for t in range(STEPS):
        for h in range(HALVES):
            apply(t, h)
    gram_first()
    apply(4, 0)
    apply(4, 1)
    sum_second(0, tiles_one)
    apply(5, 0)
    apply(5, 1)
    sum_third(0, tiles_one)
    apply(6, 0)
    apply(6, 1)
    factor_one()
    apply(7, 0, [mix_early])
    apply(7, 1, [lambda: lay_out(basis[:PANEL], turn_first, first_ref)])
    last = nn(mix_ref[...], powers[STEPS * RHS :])
    basis[PANEL + early :] = last
    both_ref[:, early:] = nt(basis[...], last)
    both_ref[PANEL + early :, :early] = nt(last, basis[PANEL : PANEL + early])

    both = both_ref[...]
    half = (PANEL + NEW) // 2
    tiles_two = half // 8
    wide = jnp.concatenate([both[:half], both[half:]], 1)
    for i in range(tiles_two):
        sum_in[1][i] = wide[i * 8 : (i + 1) * 8]
    sum_first(1, tiles_two)
    sum_second(1, tiles_two)
    sum_third(1, tiles_two)
    sum_end(1, tiles_two)
    wide = jnp.concatenate([sum_out[1][i] for i in range(tiles_two)], 0) * SCALE
    coupling = jnp.concatenate([wide[:, :NEW], wide[: PANEL - half, NEW:]], 0)
    square = wide[PANEL - half :, NEW:]
    coupling_ref[...] = coupling.T
    gram = square - tn(coupling, coupling)
    projected = basis[PANEL:] - tn(coupling, basis[:PANEL])
    upper_two, inverse_two = factor(gram)
    factor_second_ref[...] = upper_two
    lay_out(nn(inverse_two, projected), turn_second, second_ref)

    sum_sent(0, tiles_one)
    sum_sent(1, tiles_two)


def hand_over(*refs):
    n = len(refs) // 2
    copies = [pltpu.make_async_copy(refs[i], refs[n + i], refs[-1].at[i]) for i in range(n)]
    for copy in copies:
        copy.start()
    for copy in copies:
        copy.wait()


def per_device(start, stiff, convect, column_index, upwind):
    vmem = pl.BlockSpec(memory_space=pltpu.VMEM)
    hbm = pl.BlockSpec(memory_space=pl.ANY)
    f32 = jnp.float32
    rows = pltpu.VMEM((HALVES, OWN, 4, 128), f32)
    sums = lambda: [pltpu.VMEM((16, 8, 128), f32) for _ in range(2)]
    results = pl.pallas_call(
        kernel,
        out_shape=(
            jax.ShapeDtypeStruct((OWN, PANEL * BS), f32),
            jax.ShapeDtypeStruct((OWN, NEW * BS), f32),
            jax.ShapeDtypeStruct((PANEL, PANEL), f32),
            jax.ShapeDtypeStruct((NEW, PANEL), f32),
            jax.ShapeDtypeStruct((NEW, NEW), f32),
        ),
        in_specs=[vmem, hbm, hbm, hbm, hbm],
        out_specs=(vmem,) * 5,
        scratch_shapes=[
            [[pltpu.VMEM((GROUP, 4, 128), f32) for _ in range(HALVES)] for _ in range(POWERS)],
            rows,
            [rows for _ in range(POWERS)],
            [rows for _ in range(POWERS)],
            [[pltpu.VMEM((2, OWN, 4, 128), f32) for _ in range(HALVES)] for _ in range(POWERS)],
            pltpu.VMEM((OWN, BS, SLOTS * BS), f32),
            pltpu.VMEM((OWN, BS, BS), f32),
            pltpu.VMEM((OWN, BS, 8 * BS), f32),
            pltpu.VMEM((OWN, BS, 2 * BS), f32),
            pltpu.VMEM((OWN, PART, BS), f32),
            pltpu.VMEM((ALL, WIDE), f32),
            pltpu.VMEM((PANEL + NEW, WIDE), f32),
            pltpu.VMEM((RHS, PANEL), f32),
            pltpu.VMEM((PANEL + NEW, NEW), f32),
            pltpu.VMEM((PANEL, OWN, 2 * BS), f32),
            pltpu.VMEM((NEW, OWN, 2 * BS), f32),
            pltpu.VMEM((2, OWN, SLOTS), jnp.int32),
            pltpu.SMEM((OWN, SLOTS), jnp.int32),
            pltpu.SMEM((OWN, SLOTS), jnp.int32),
            pltpu.SMEM((OWN, SLOTS), jnp.int32),
            pltpu.SMEM((OWN, SLOTS), jnp.int32),
            sums(),
            sums(),
            sums(),
            sums(),
            pltpu.SemaphoreType.DMA((POWERS, HALVES)),
            pltpu.SemaphoreType.DMA((POWERS, HALVES)),
            pltpu.SemaphoreType.DMA((POWERS, HALVES, 2)),
            pltpu.SemaphoreType.DMA((POWERS, HALVES, 2)),
            pltpu.SemaphoreType.DMA((2,)),
            pltpu.SemaphoreType.DMA((2,)),
            pltpu.SemaphoreType.DMA((6,)),
            pltpu.SemaphoreType.DMA((2, 3)),
            pltpu.SemaphoreType.DMA((2, 3)),
        ],
        compiler_params=pltpu.CompilerParams(
            collective_id=0, has_side_effects=True, vmem_limit_bytes=56 << 20
        ),
    )(start, stiff, convect, column_index, upwind)
    first, second, factor_first, coupling, factor_second = pl.pallas_call(
        hand_over,
        out_shape=tuple(jax.ShapeDtypeStruct(x.shape, f32) for x in results),
        in_specs=[vmem] * len(results),
        out_specs=(hbm,) * len(results),
        scratch_shapes=[pltpu.SemaphoreType.DMA((len(results),))],
    )(*results)
    return first, second, factor_first, coupling.T, factor_second


def solution(mesh):
    return jax.shard_map(
        per_device,
        mesh=mesh,
        in_specs=(
            P(("row", "col"), None),
            P(("row", "col"), None, None),
            P(("row", "col"), None, None),
            P(("row", "col"), None),
            P(("row", "col"), None),
        ),
        out_specs=(P(("row", "col"), None), P(("row", "col"), None), P(), P(), P()),
        check_vma=False,
    )
```

```python
import functools

import jax
import jax.numpy as jnp
from jax import lax
from jax.experimental import pallas as pl
from jax.experimental.pallas import tpu as pltpu
from jax.sharding import PartitionSpec as P

MESH = pl.DeviceIdType.MESH
HIGHEST = lax.Precision.HIGHEST
STEPS = 4
POWERS = 2 * STEPS
BS = 64
RHS = 16
SLOTS = 9
OWN = 8
COLS = 16
SIDE = 4
ROWS_AXIS = 16
GROUP = OWN * COLS
PANEL = (STEPS + 1) * RHS
NEW = STEPS * RHS
ALL = (POWERS + 1) * RHS
WIDE = OWN * BS
HALVES = 2
PART = RHS // HALVES
SCALE = 1.0 / (GROUP * ROWS_AXIS * BS)


def dot(a, b, contract):
    return lax.dot_general(
        a, b, (contract, ((), ())), precision=HIGHEST, preferred_element_type=jnp.float32
    )


def nt(a, b):
    return dot(a, b, ((1,), (1,)))


def nn(a, b):
    return dot(a, b, ((1,), (0,)))


def tn(a, b):
    return dot(a, b, ((0,), (0,)))


def parts(x):
    high = x.astype(jnp.bfloat16).astype(jnp.float32)
    rest = x - high
    middle = rest.astype(jnp.bfloat16).astype(jnp.float32)
    return [high, middle, rest - middle]


def weight_parts(x):
    return jnp.concatenate(parts(x), 0).astype(jnp.bfloat16)


def product(near, weights):
    left = jnp.concatenate(parts(near) + [jnp.zeros_like(near)], 0).astype(jnp.bfloat16)
    every = lax.dot_general(left, weights, (((1,), (1,)), ((), ())), preferred_element_type=jnp.float32)
    total = every[16:24] + every[8:16] + every[:8]
    return total[:, 2 * BS :] + total[:, BS : 2 * BS] + total[:, :BS]


def local_row(index):
    return lax.bitwise_and(index, GROUP - 1)


def side_by_side(a, b):
    low = lax.broadcasted_iota(jnp.int32, a.shape, 1) < BS
    top = jnp.where(low, a, pltpu.roll(b, BS, 1))
    bottom = jnp.where(low, pltpu.roll(a, BS, 1), b)
    return jnp.concatenate([top, bottom], 0)


def factor(gram):
    n = gram.shape[0]
    tiles = n // 8
    shape = (8, n)
    sub = lax.broadcasted_iota(jnp.int32, shape, 0)
    lane = lax.broadcasted_iota(jnp.int32, shape, 1)
    left = [gram[8 * i : 8 * i + 8] for i in range(tiles)]
    right = [jnp.where(lane == sub + 8 * i, 1.0, 0.0) for i in range(tiles)]
    upper, inverse = [], []
    for k in range(tiles):
        columns = [
            [jnp.broadcast_to(left[i][:, 8 * k + j : 8 * k + j + 1], shape) if i >= k else None for i in range(tiles)]
            for j in range(8)
        ]
        pivots = jnp.ones(shape, jnp.float32)
        for j in range(8):
            pivot = columns[j][k][j : j + 1]
            scale = 1.0 / pivot
            pivots = jnp.where(sub == j, pivot, pivots)
            across = [columns[c][k][j : j + 1] for c in range(8)]
            row_left, row_right = left[k][j : j + 1], right[k][j : j + 1]
            for i in range(k, tiles):
                gain = columns[j][i] * scale
                if i == k:
                    gain = jnp.where(sub > j, gain, 0.0)
                for c in range(j + 1, 8):
                    columns[c][i] = columns[c][i] - gain * across[c]
                left[i] = left[i] - gain * row_left
                right[i] = right[i] - gain * row_right
        scale = lax.rsqrt(pivots)
        scale = scale * (1.5 - 0.5 * pivots * scale * scale)
        upper.append(jnp.where(lane >= sub + 8 * k, left[k], 0.0) * scale)
        inverse.append(right[k] * scale)
    return jnp.concatenate(upper, 0), jnp.concatenate(inverse, 0)


def kernel(
    start_ref, stiff_hbm, convect_hbm, index_hbm, upwind_hbm,
    first_ref, second_ref, factor_first_ref, coupling_ref, factor_second_ref,
    field, start_tiles, rows_twin, rows_far, give, stiff_ref, convect_ref, w_main, w_far, partial, powers, basis, mix_ref, both_ref, turn_first, turn_second,
    index_in, index_ref, upwind_ref, index_twin, index_far,
    sum_in, sum_a, sum_b, sum_out,
    send_sem, recv_sem, far_send, far_recv, index_send, index_recv, local_sem,
    sum_send, sum_recv,
):
    row = lax.axis_index("row")
    col = lax.axis_index("col")
    away = lambda i: min(i, SIDE - i)
    steps = sorted(
        ((i, j) for i in range(SIDE) for j in range(SIDE) if i or j), key=lambda p: -away(p[0]) - away(p[1])
    )
    sector_peers = [
        (row, lax.rem(col // SIDE + i, SIDE) * SIDE + lax.rem(lax.rem(col, SIDE) + j, SIDE)) for i, j in steps
    ]
    ring = sorted(range(1, ROWS_AXIS), key=lambda i: -min(i, ROWS_AXIS - i))
    row_peers = [(lax.rem(row + i, ROWS_AXIS), col) for i in ring]
    odd = lax.rem(row, 2)
    twin = (row + 1 - 2 * odd, col)
    far = (lax.rem(row + ROWS_AXIS - 1 + 2 * odd, ROWS_AXIS), col)
    slot_twin, slot_far = SLOTS - 2 + odd, SLOTS - 1 - odd

    barrier = pltpu.get_barrier_semaphore()
    for peer in sector_peers + [twin, far]:
        pl.semaphore_signal(barrier, inc=1, device_id=peer, device_id_type=MESH)
    loads = [
        pltpu.make_async_copy(src, dst, local_sem.at[i])
        for i, (src, dst) in enumerate(
            [(index_hbm, index_ref), (upwind_hbm, upwind_ref), (convect_hbm, convect_ref), (stiff_hbm, stiff_ref)]
        )
    ]
    for copy in loads:
        copy.start()
    own = pl.ds(col * OWN, OWN)
    for h in range(HALVES):
        for m in range(4):
            c = (h * PART + m) * BS
            start_tiles[h, :, m, :] = jnp.concatenate([start_ref[:, c : c + BS], start_ref[:, c + 4 * BS : c + 5 * BS]], 1)
        field[0][h][own] = start_tiles[h]
    pl.semaphore_wait(barrier, COLS + 1)

    pending = []

    def push(src, dst, send, recv, peer):
        copy = pltpu.make_async_remote_copy(
            src_ref=src, dst_ref=dst, send_sem=send, recv_sem=recv, device_id=peer, device_id_type=MESH
        )
        copy.start()
        return copy

    def arrived(ref, sem):
        pltpu.make_async_copy(ref, ref, sem).wait()

    def others(t, h):
        return field[t][h].at[pl.ds(0, GROUP - OWN)]

    def spread(t, h):
        mine = field[t][h].at[own]
        for peer in sector_peers:
            push(mine, mine, send_sem.at[t, h], recv_sem.at[t, h], peer)

    def keep(t, h, rows):
        for b in range(0, OWN, 2):
            powers[t * RHS + h * PART : t * RHS + (h + 1) * PART, b * BS : (b + 2) * BS] = rows(b)

    def sum_first(s, tiles):
        for peer in sector_peers:
            @pl.when(peer[1] < tiles)
            def _(peer=peer):
                push(sum_in[s].at[peer[1]], sum_a[s].at[col], sum_send.at[s, 0], sum_recv.at[s, 0], peer)

    def sum_second(s, tiles):
        @pl.when(col < tiles)
        def _():
            sum_a[s][col] = sum_in[s][col]
            arrived(sum_a[s].at[pl.ds(0, COLS - 1)], sum_recv.at[s, 0])
            sum_b[s][row] = total_of(sum_a[s])
            for peer in row_peers:
                push(sum_b[s].at[row], sum_b[s].at[row], sum_send.at[s, 1], sum_recv.at[s, 1], peer)

    def sum_third(s, tiles):
        @pl.when(col < tiles)
        def _():
            arrived(sum_b[s].at[pl.ds(0, ROWS_AXIS - 1)], sum_recv.at[s, 1])
            sum_out[s][col] = total_of(sum_b[s])
            for peer in sector_peers:
                push(sum_out[s].at[col], sum_out[s].at[col], sum_send.at[s, 2], sum_recv.at[s, 2], peer)

    def sum_end(s, tiles):
        @pl.when(col < tiles)
        def _():
            arrived(sum_out[s].at[pl.ds(0, tiles - 1)], sum_recv.at[s, 2])

        @pl.when(col >= tiles)
        def _():
            arrived(sum_out[s].at[pl.ds(0, tiles)], sum_recv.at[s, 2])

    def sum_sent(s, tiles):
        @pl.when(col < tiles)
        def _():
            arrived(sum_in[s].at[pl.ds(0, tiles - 1)], sum_send.at[s, 0])
            arrived(sum_b[s].at[pl.ds(0, ROWS_AXIS - 1)], sum_send.at[s, 1])
            arrived(sum_out[s].at[pl.ds(0, COLS - 1)], sum_send.at[s, 2])

        @pl.when(col >= tiles)
        def _():
            arrived(sum_in[s].at[pl.ds(0, tiles)], sum_send.at[s, 0])

    def total_of(ref):
        terms = [ref[i] for i in range(16)]
        while len(terms) > 1:
            terms = [terms[i] + terms[i + 1] for i in range(0, len(terms), 2)]
        return terms[0]

    for h in range(HALVES):
        spread(0, h)
    pending.append(push(index_hbm, index_in.at[0], index_send.at[0], index_recv.at[0], twin))
    pending.append(push(index_hbm, index_in.at[1], index_send.at[1], index_recv.at[1], far))
    for h in range(HALVES):
        keep(0, h, lambda b: side_by_side(start_tiles[h, b], start_tiles[h, b + 1]))

    for copy in loads:
        copy.wait()
    for b in range(OWN):
        flags = [upwind_ref[b, j].astype(jnp.float32) for j in range(SLOTS)]
        total = functools.reduce(lambda x, y: x + y, flags)
        flags[0] = flags[0] - total
        convect = convect_ref[b]
        blocks = [stiff_ref[b, :, j * BS : (j + 1) * BS] + flags[j] * convect for j in range(SLOTS)]
        blocks.insert(7, jnp.zeros_like(convect))
        w_main[b] = weight_parts(jnp.concatenate(blocks[:8], 1))
        near_far = [jnp.where(odd == 0, blocks[9], blocks[8]), jnp.where(odd == 0, blocks[8], blocks[9])]
        w_far[b] = weight_parts(jnp.concatenate(near_far, 1))

    arrived(index_in.at[0], index_recv.at[0])
    arrived(index_in.at[1], index_recv.at[1])
    local = [
        pltpu.make_async_copy(index_in.at[0], index_twin, local_sem.at[4]),
        pltpu.make_async_copy(index_in.at[1], index_far, local_sem.at[5]),
    ]
    for copy in local:
        copy.start()
    for copy in local:
        copy.wait()

    def apply(t, h, beside=()):
        f = field[t][h]
        arrived(others(t, h), recv_sem.at[t, h])
        for b in range(OWN):
            give[t][h][0, b] = f[local_row(index_far[b, slot_far])]
        pending.append(push(give[t][h].at[0], rows_far[t].at[h], far_send.at[t, h, 0], far_recv.at[t, h, 0], far))
        for b in range(OWN):
            give[t][h][1, b] = f[local_row(index_twin[b, slot_twin])]
        pending.append(push(give[t][h].at[1], rows_twin[t].at[h], far_send.at[t, h, 1], far_recv.at[t, h, 1], twin))
        for b in range(OWN):
            tiles = [f[col * OWN + b]] + [f[local_row(index_ref[b, j])] for j in range(1, 7)]
            tiles.append(jnp.zeros_like(tiles[0]))
            near = jnp.concatenate([side_by_side(tiles[j], tiles[j + 1]) for j in range(0, 8, 2)], 1)
            partial[b] = product(near, w_main[b])
        arrived(rows_twin[t].at[h], far_recv.at[t, h, 1])
        for call in beside:
            call()
        arrived(rows_far[t].at[h], far_recv.at[t, h, 0])
        results = []
        for b in range(OWN):
            near = side_by_side(rows_twin[t][h, b], rows_far[t][h, b])
            result = partial[b] + product(near, w_far[b])
            results.append(result)
            if t + 1 < POWERS:
                field[t + 1][h][col * OWN + b] = jnp.concatenate([result[:4], result[4:]], 1)
        if t + 1 < POWERS:
            spread(t + 1, h)
        keep(t + 1, h, lambda b: jnp.concatenate([results[b], results[b + 1]], 1))
        arrived(others(t, h), send_sem.at[t, h])
        for copy in pending:
            copy.wait_send()
        pending.clear()

    def gram_first():
        panel = powers[:PANEL, :]
        gram = nt(panel, panel)
        wide = jnp.concatenate([gram, jnp.zeros((PANEL, 128 - PANEL), jnp.float32)], 1)
        for i in range(tiles_one):
            sum_in[0][i] = wide[i * 8 : (i + 1) * 8]
        sum_first(0, tiles_one)

    def factor_one():
        sum_end(0, tiles_one)
        gram = jnp.concatenate([sum_out[0][i] for i in range(tiles_one)], 0)[:, :PANEL] * SCALE
        upper_one, inverse_one = factor(gram)
        factor_first_ref[...] = upper_one
        basis[:PANEL] = nn(inverse_one, powers[:PANEL, :])
        mix_ref[...] = inverse_one[PANEL - RHS :]

    def mix_early():
        for k in range(1, STEPS):
            basis[PANEL + (k - 1) * RHS : PANEL + k * RHS] = nn(mix_ref[...], powers[k * RHS : k * RHS + PANEL])
        both_ref[: PANEL + early, :early] = nt(basis[: PANEL + early], basis[PANEL : PANEL + early])

    def lay_out(value, turn, out_ref):
        n = value.shape[0]
        low = lax.broadcasted_iota(jnp.int32, (OWN, 2 * BS), 1) < BS
        for b in range(OWN):
            pair = value[:, b // 2 * 2 * BS : (b // 2 + 1) * 2 * BS]
            turn[:, b, :] = pair if b % 2 == 0 else pltpu.roll(pair, BS, 1)
        for p in range(0, n, 2):
            out_ref[:, p * BS : (p + 2) * BS] = jnp.where(low, turn[p], pltpu.roll(turn[p + 1], BS, 1))

    early = NEW - RHS
    tiles_one = PANEL // 8
    for t in range(STEPS):
        for h in range(HALVES):
            apply(t, h)
    gram_first()
    apply(4, 0)
    apply(4, 1)
    sum_second(0, tiles_one)
    apply(5, 0)
    apply(5, 1)
    sum_third(0, tiles_one)
    apply(6, 0)
    apply(6, 1)
    factor_one()
    apply(7, 0, [mix_early])
    apply(7, 1, [lambda: lay_out(basis[:PANEL], turn_first, first_ref)])
    last = nn(mix_ref[...], powers[STEPS * RHS :])
    basis[PANEL + early :] = last
    both_ref[:, early:] = nt(basis[...], last)
    both_ref[PANEL + early :, :early] = nt(last, basis[PANEL : PANEL + early])

    both = both_ref[...]
    half = (PANEL + NEW) // 2
    tiles_two = half // 8
    wide = jnp.concatenate([both[:half], both[half:]], 1)
    for i in range(tiles_two):
        sum_in[1][i] = wide[i * 8 : (i + 1) * 8]
    sum_first(1, tiles_two)
    sum_second(1, tiles_two)
    sum_third(1, tiles_two)
    sum_end(1, tiles_two)
    wide = jnp.concatenate([sum_out[1][i] for i in range(tiles_two)], 0) * SCALE
    coupling = jnp.concatenate([wide[:, :NEW], wide[: PANEL - half, NEW:]], 0)
    square = wide[PANEL - half :, NEW:]
    coupling_ref[...] = coupling.T
    gram = square - tn(coupling, coupling)
    projected = basis[PANEL:] - tn(coupling, basis[:PANEL])
    upper_two, inverse_two = factor(gram)
    factor_second_ref[...] = upper_two
    lay_out(nn(inverse_two, projected), turn_second, second_ref)

    sum_sent(0, tiles_one)
    sum_sent(1, tiles_two)


def hand_over(*refs):
    n = len(refs) // 2
    copies = [pltpu.make_async_copy(refs[i], refs[n + i], refs[-1].at[i]) for i in range(n)]
    for copy in copies:
        copy.start()
    for copy in copies:
        copy.wait()


def per_device(start, stiff, convect, column_index, upwind):
    vmem = pl.BlockSpec(memory_space=pltpu.VMEM)
    hbm = pl.BlockSpec(memory_space=pl.ANY)
    f32 = jnp.float32
    rows = pltpu.VMEM((HALVES, OWN, 4, 128), f32)
    sums = lambda: [pltpu.VMEM((16, 8, 128), f32) for _ in range(2)]
    results = pl.pallas_call(
        kernel,
        out_shape=(
            jax.ShapeDtypeStruct((OWN, PANEL * BS), f32),
            jax.ShapeDtypeStruct((OWN, NEW * BS), f32),
            jax.ShapeDtypeStruct((PANEL, PANEL), f32),
            jax.ShapeDtypeStruct((NEW, PANEL), f32),
            jax.ShapeDtypeStruct((NEW, NEW), f32),
        ),
        in_specs=[vmem, hbm, hbm, hbm, hbm],
        out_specs=(vmem,) * 5,
        scratch_shapes=[
            [[pltpu.VMEM((GROUP, 4, 128), f32) for _ in range(HALVES)] for _ in range(POWERS)],
            rows,
            [rows for _ in range(POWERS)],
            [rows for _ in range(POWERS)],
            [[pltpu.VMEM((2, OWN, 4, 128), f32) for _ in range(HALVES)] for _ in range(POWERS)],
            pltpu.VMEM((OWN, BS, SLOTS * BS), f32),
            pltpu.VMEM((OWN, BS, BS), f32),
            pltpu.VMEM((OWN, 3 * BS, 8 * BS), jnp.bfloat16),
            pltpu.VMEM((OWN, 3 * BS, 2 * BS), jnp.bfloat16),
            pltpu.VMEM((OWN, PART, BS), f32),
            pltpu.VMEM((ALL, WIDE), f32),
            pltpu.VMEM((PANEL + NEW, WIDE), f32),
            pltpu.VMEM((RHS, PANEL), f32),
            pltpu.VMEM((PANEL + NEW, NEW), f32),
            pltpu.VMEM((PANEL, OWN, 2 * BS), f32),
            pltpu.VMEM((NEW, OWN, 2 * BS), f32),
            pltpu.VMEM((2, OWN, SLOTS), jnp.int32),
            pltpu.SMEM((OWN, SLOTS), jnp.int32),
            pltpu.SMEM((OWN, SLOTS), jnp.int32),
            pltpu.SMEM((OWN, SLOTS), jnp.int32),
            pltpu.SMEM((OWN, SLOTS), jnp.int32),
            sums(),
            sums(),
            sums(),
            sums(),
            pltpu.SemaphoreType.DMA((POWERS, HALVES)),
            pltpu.SemaphoreType.DMA((POWERS, HALVES)),
            pltpu.SemaphoreType.DMA((POWERS, HALVES, 2)),
            pltpu.SemaphoreType.DMA((POWERS, HALVES, 2)),
            pltpu.SemaphoreType.DMA((2,)),
            pltpu.SemaphoreType.DMA((2,)),
            pltpu.SemaphoreType.DMA((6,)),
            pltpu.SemaphoreType.DMA((2, 3)),
            pltpu.SemaphoreType.DMA((2, 3)),
        ],
        compiler_params=pltpu.CompilerParams(
            collective_id=0, has_side_effects=True, vmem_limit_bytes=56 << 20
        ),
    )(start, stiff, convect, column_index, upwind)
    first, second, factor_first, coupling, factor_second = pl.pallas_call(
        hand_over,
        out_shape=tuple(jax.ShapeDtypeStruct(x.shape, f32) for x in results),
        in_specs=[vmem] * len(results),
        out_specs=(hbm,) * len(results),
        scratch_shapes=[pltpu.SemaphoreType.DMA((len(results),))],
    )(*results)
    return first, second, factor_first, coupling.T, factor_second


def solution(mesh):
    return jax.shard_map(
        per_device,
        mesh=mesh,
        in_specs=(
            P(("row", "col"), None),
            P(("row", "col"), None, None),
            P(("row", "col"), None, None),
            P(("row", "col"), None),
            P(("row", "col"), None),
        ),
        out_specs=(P(("row", "col"), None), P(("row", "col"), None), P(), P(), P()),
        check_vma=False,
    )
```

```python
import functools

import jax
import jax.numpy as jnp
from jax import lax
from jax.experimental import pallas as pl
from jax.experimental.pallas import tpu as pltpu
from jax.sharding import PartitionSpec as P

MESH = pl.DeviceIdType.MESH
HIGHEST = lax.Precision.HIGHEST
STEPS = 4
POWERS = 2 * STEPS
BS = 64
RHS = 16
SLOTS = 9
OWN = 8
COLS = 16
SIDE = 4
ROWS_AXIS = 16
GROUP = OWN * COLS
PANEL = (STEPS + 1) * RHS
NEW = STEPS * RHS
ALL = (POWERS + 1) * RHS
WIDE = OWN * BS
HALVES = 2
PART = RHS // HALVES
SCALE = 1.0 / (GROUP * ROWS_AXIS * BS)


def dot(a, b, contract):
    return lax.dot_general(
        a, b, (contract, ((), ())), precision=HIGHEST, preferred_element_type=jnp.float32
    )


def nt(a, b):
    return dot(a, b, ((1,), (1,)))


def nn(a, b):
    return dot(a, b, ((1,), (0,)))


def tn(a, b):
    return dot(a, b, ((0,), (0,)))


def parts(x):
    high = x.astype(jnp.bfloat16).astype(jnp.float32)
    rest = x - high
    middle = rest.astype(jnp.bfloat16).astype(jnp.float32)
    return [high, middle, rest - middle]


def weight_parts(x):
    return jnp.concatenate(parts(x), 0).astype(jnp.bfloat16)


def product(near, weights):
    left = jnp.concatenate(parts(near) + [jnp.zeros_like(near)], 0).astype(jnp.bfloat16)
    every = lax.dot_general(left, weights, (((1,), (1,)), ((), ())), preferred_element_type=jnp.float32)
    total = every[16:24] + every[8:16] + every[:8]
    return total[:, 2 * BS :] + total[:, BS : 2 * BS] + total[:, :BS]


def local_row(index):
    return lax.bitwise_and(index, GROUP - 1)


def side_by_side(a, b):
    low = lax.broadcasted_iota(jnp.int32, a.shape, 1) < BS
    top = jnp.where(low, a, pltpu.roll(b, BS, 1))
    bottom = jnp.where(low, pltpu.roll(a, BS, 1), b)
    return jnp.concatenate([top, bottom], 0)


def factor(gram):
    n = gram.shape[0]
    tiles = n // 8
    shape = (8, n)
    sub = lax.broadcasted_iota(jnp.int32, shape, 0)
    lane = lax.broadcasted_iota(jnp.int32, shape, 1)
    left = [gram[8 * i : 8 * i + 8] for i in range(tiles)]
    right = [jnp.where(lane == sub + 8 * i, 1.0, 0.0) for i in range(tiles)]
    upper, inverse = [], []
    for k in range(tiles):
        columns = [
            [jnp.broadcast_to(left[i][:, 8 * k + j : 8 * k + j + 1], shape) if i >= k else None for i in range(tiles)]
            for j in range(8)
        ]
        pivots = jnp.ones(shape, jnp.float32)
        for j in range(8):
            pivot = columns[j][k][j : j + 1]
            scale = 1.0 / pivot
            pivots = jnp.where(sub == j, pivot, pivots)
            across = [columns[c][k][j : j + 1] for c in range(8)]
            row_left, row_right = left[k][j : j + 1], right[k][j : j + 1]
            for i in range(k, tiles):
                gain = columns[j][i] * scale
                if i == k:
                    gain = jnp.where(sub > j, gain, 0.0)
                for c in range(j + 1, 8):
                    columns[c][i] = columns[c][i] - gain * across[c]
                left[i] = left[i] - gain * row_left
                right[i] = right[i] - gain * row_right
        scale = lax.rsqrt(pivots)
        scale = scale * (1.5 - 0.5 * pivots * scale * scale)
        upper.append(jnp.where(lane >= sub + 8 * k, left[k], 0.0) * scale)
        inverse.append(right[k] * scale)
    return jnp.concatenate(upper, 0), jnp.concatenate(inverse, 0)


def kernel(
    start_ref, stiff_hbm, convect_hbm, index_hbm, upwind_hbm,
    first_ref, second_ref, factor_first_ref, coupling_ref, factor_second_ref,
    field, start_tiles, rows_twin, rows_far, give, stiff_ref, convect_ref, w_main, w_far, partial, powers, basis, mix_ref, both_ref, turn_first, turn_second,
    index_in, index_ref, upwind_ref, index_twin, index_far,
    sum_in, sum_a, sum_b, sum_out,
    send_sem, recv_sem, far_send, far_recv, index_send, index_recv, local_sem,
    sum_send, sum_recv,
):
    row = lax.axis_index("row")
    col = lax.axis_index("col")
    away = lambda i: min(i, SIDE - i)
    steps = sorted(
        ((i, j) for i in range(SIDE) for j in range(SIDE) if i or j), key=lambda p: -away(p[0]) - away(p[1])
    )
    sector_peers = [
        (row, lax.rem(col // SIDE + i, SIDE) * SIDE + lax.rem(lax.rem(col, SIDE) + j, SIDE)) for i, j in steps
    ]
    ring = sorted(range(1, ROWS_AXIS), key=lambda i: -min(i, ROWS_AXIS - i))
    row_peers = [(lax.rem(row + i, ROWS_AXIS), col) for i in ring]
    odd = lax.rem(row, 2)
    twin = (row + 1 - 2 * odd, col)
    far = (lax.rem(row + ROWS_AXIS - 1 + 2 * odd, ROWS_AXIS), col)
    slot_twin, slot_far = SLOTS - 2 + odd, SLOTS - 1 - odd

    barrier = pltpu.get_barrier_semaphore()
    for peer in sector_peers + [twin, far]:
        pl.semaphore_signal(barrier, inc=1, device_id=peer, device_id_type=MESH)
    loads = [
        pltpu.make_async_copy(src, dst, local_sem.at[i])
        for i, (src, dst) in enumerate(
            [(index_hbm, index_ref), (upwind_hbm, upwind_ref), (convect_hbm, convect_ref), (stiff_hbm, stiff_ref)]
        )
    ]
    for copy in loads:
        copy.start()
    own = pl.ds(col * OWN, OWN)
    for h in range(HALVES):
        for m in range(4):
            c = (h * PART + m) * BS
            start_tiles[h, :, m, :] = jnp.concatenate([start_ref[:, c : c + BS], start_ref[:, c + 4 * BS : c + 5 * BS]], 1)
        field[0][h][own] = start_tiles[h]
    pl.semaphore_wait(barrier, COLS + 1)

    pending = []

    def push(src, dst, send, recv, peer):
        copy = pltpu.make_async_remote_copy(
            src_ref=src, dst_ref=dst, send_sem=send, recv_sem=recv, device_id=peer, device_id_type=MESH
        )
        copy.start()
        return copy

    def arrived(ref, sem):
        pltpu.make_async_copy(ref, ref, sem).wait()

    def others(t, h):
        return field[t][h].at[pl.ds(0, GROUP - OWN)]

    def spread(t, h):
        mine = field[t][h].at[own]
        for peer in sector_peers:
            push(mine, mine, send_sem.at[t, h], recv_sem.at[t, h], peer)

    def keep(t, h, rows):
        for b in range(0, OWN, 2):
            powers[t * RHS + h * PART : t * RHS + (h + 1) * PART, b * BS : (b + 2) * BS] = rows(b)

    def sum_first(s, tiles):
        for peer in sector_peers:
            @pl.when(peer[1] < tiles)
            def _(peer=peer):
                push(sum_in[s].at[peer[1]], sum_a[s].at[col], sum_send.at[s, 0], sum_recv.at[s, 0], peer)

    def sum_second(s, tiles):
        @pl.when(col < tiles)
        def _():
            sum_a[s][col] = sum_in[s][col]
            arrived(sum_a[s].at[pl.ds(0, COLS - 1)], sum_recv.at[s, 0])
            sum_b[s][row] = total_of(sum_a[s])
            for peer in row_peers:
                push(sum_b[s].at[row], sum_b[s].at[row], sum_send.at[s, 1], sum_recv.at[s, 1], peer)

    def sum_third(s, tiles):
        @pl.when(col < tiles)
        def _():
            arrived(sum_b[s].at[pl.ds(0, ROWS_AXIS - 1)], sum_recv.at[s, 1])
            sum_out[s][col] = total_of(sum_b[s])
            for peer in sector_peers:
                push(sum_out[s].at[col], sum_out[s].at[col], sum_send.at[s, 2], sum_recv.at[s, 2], peer)

    def sum_end(s, tiles):
        @pl.when(col < tiles)
        def _():
            arrived(sum_out[s].at[pl.ds(0, tiles - 1)], sum_recv.at[s, 2])

        @pl.when(col >= tiles)
        def _():
            arrived(sum_out[s].at[pl.ds(0, tiles)], sum_recv.at[s, 2])

    def sum_sent(s, tiles):
        @pl.when(col < tiles)
        def _():
            arrived(sum_in[s].at[pl.ds(0, tiles - 1)], sum_send.at[s, 0])
            arrived(sum_b[s].at[pl.ds(0, ROWS_AXIS - 1)], sum_send.at[s, 1])
            arrived(sum_out[s].at[pl.ds(0, COLS - 1)], sum_send.at[s, 2])

        @pl.when(col >= tiles)
        def _():
            arrived(sum_in[s].at[pl.ds(0, tiles)], sum_send.at[s, 0])

    def total_of(ref):
        terms = [ref[i] for i in range(16)]
        while len(terms) > 1:
            terms = [terms[i] + terms[i + 1] for i in range(0, len(terms), 2)]
        return terms[0]

    for h in range(HALVES):
        spread(0, h)
    pending.append(push(index_hbm, index_in.at[0], index_send.at[0], index_recv.at[0], twin))
    pending.append(push(index_hbm, index_in.at[1], index_send.at[1], index_recv.at[1], far))
    for h in range(HALVES):
        keep(0, h, lambda b: side_by_side(start_tiles[h, b], start_tiles[h, b + 1]))

    for copy in loads:
        copy.wait()
    for b in range(OWN):
        flags = [upwind_ref[b, j].astype(jnp.float32) for j in range(SLOTS)]
        total = functools.reduce(lambda x, y: x + y, flags)
        flags[0] = flags[0] - total
        convect = convect_ref[b]
        blocks = [stiff_ref[b, :, j * BS : (j + 1) * BS] + flags[j] * convect for j in range(SLOTS)]
        blocks.insert(7, jnp.zeros_like(convect))
        w_main[b] = weight_parts(jnp.concatenate(blocks[:8], 1))
        near_far = [jnp.where(odd == 0, blocks[9], blocks[8]), jnp.where(odd == 0, blocks[8], blocks[9])]
        w_far[b] = weight_parts(jnp.concatenate(near_far, 1))

    arrived(index_in.at[0], index_recv.at[0])
    arrived(index_in.at[1], index_recv.at[1])
    local = [
        pltpu.make_async_copy(index_in.at[0], index_twin, local_sem.at[4]),
        pltpu.make_async_copy(index_in.at[1], index_far, local_sem.at[5]),
    ]
    for copy in local:
        copy.start()
    for copy in local:
        copy.wait()

    def apply(t, h, beside=()):
        f = field[t][h]
        arrived(others(t, h), recv_sem.at[t, h])
        for b in range(OWN):
            give[t][h][0, b] = f[local_row(index_far[b, slot_far])]
        pending.append(push(give[t][h].at[0], rows_far[t].at[h], far_send.at[t, h, 0], far_recv.at[t, h, 0], far))
        for b in range(OWN):
            give[t][h][1, b] = f[local_row(index_twin[b, slot_twin])]
        pending.append(push(give[t][h].at[1], rows_twin[t].at[h], far_send.at[t, h, 1], far_recv.at[t, h, 1], twin))
        for b in range(OWN):
            tiles = [f[col * OWN + b]] + [f[local_row(index_ref[b, j])] for j in range(1, 7)]
            tiles.append(jnp.zeros_like(tiles[0]))
            near = jnp.concatenate([side_by_side(tiles[j], tiles[j + 1]) for j in range(0, 8, 2)], 1)
            partial[b] = product(near, w_main[b])
        arrived(rows_twin[t].at[h], far_recv.at[t, h, 1])
        for call in beside:
            call()
        arrived(rows_far[t].at[h], far_recv.at[t, h, 0])
        results = []
        for b in range(OWN):
            near = side_by_side(rows_twin[t][h, b], rows_far[t][h, b])
            result = partial[b] + product(near, w_far[b])
            results.append(result)
        for b, result in enumerate(results):
            if t + 1 < POWERS:
                field[t + 1][h][col * OWN + b] = jnp.concatenate([result[:4], result[4:]], 1)
        if t + 1 < POWERS:
            spread(t + 1, h)
        keep(t + 1, h, lambda b: jnp.concatenate([results[b], results[b + 1]], 1))
        arrived(others(t, h), send_sem.at[t, h])
        for copy in pending:
            copy.wait_send()
        pending.clear()

    def gram_first():
        panel = powers[:PANEL, :]
        gram = nt(panel, panel)
        wide = jnp.concatenate([gram, jnp.zeros((PANEL, 128 - PANEL), jnp.float32)], 1)
        for i in range(tiles_one):
            sum_in[0][i] = wide[i * 8 : (i + 1) * 8]
        sum_first(0, tiles_one)

    def factor_one():
        sum_end(0, tiles_one)
        gram = jnp.concatenate([sum_out[0][i] for i in range(tiles_one)], 0)[:, :PANEL] * SCALE
        upper_one, inverse_one = factor(gram)
        factor_first_ref[...] = upper_one
        basis[:PANEL] = nn(inverse_one, powers[:PANEL, :])
        mix_ref[...] = inverse_one[PANEL - RHS :]

    def mix_early():
        for k in range(1, STEPS):
            basis[PANEL + (k - 1) * RHS : PANEL + k * RHS] = nn(mix_ref[...], powers[k * RHS : k * RHS + PANEL])
        both_ref[: PANEL + early, :early] = nt(basis[: PANEL + early], basis[PANEL : PANEL + early])

    def lay_out(value, turn, out_ref):
        n = value.shape[0]
        low = lax.broadcasted_iota(jnp.int32, (OWN, 2 * BS), 1) < BS
        for b in range(OWN):
            pair = value[:, b // 2 * 2 * BS : (b // 2 + 1) * 2 * BS]
            turn[:, b, :] = pair if b % 2 == 0 else pltpu.roll(pair, BS, 1)
        for p in range(0, n, 2):
            out_ref[:, p * BS : (p + 2) * BS] = jnp.where(low, turn[p], pltpu.roll(turn[p + 1], BS, 1))

    early = NEW - RHS
    tiles_one = PANEL // 8
    for t in range(STEPS):
        for h in range(HALVES):
            apply(t, h)
    gram_first()
    apply(4, 0)
    apply(4, 1)
    sum_second(0, tiles_one)
    apply(5, 0)
    apply(5, 1)
    sum_third(0, tiles_one)
    apply(6, 0)
    apply(6, 1)
    factor_one()
    apply(7, 0, [mix_early])
    apply(7, 1, [lambda: lay_out(basis[:PANEL], turn_first, first_ref)])
    last = nn(mix_ref[...], powers[STEPS * RHS :])
    basis[PANEL + early :] = last
    both_ref[:, early:] = nt(basis[...], last)
    both_ref[PANEL + early :, :early] = nt(last, basis[PANEL : PANEL + early])

    both = both_ref[...]
    half = (PANEL + NEW) // 2
    tiles_two = half // 8
    wide = jnp.concatenate([both[:half], both[half:]], 1)
    for i in range(tiles_two):
        sum_in[1][i] = wide[i * 8 : (i + 1) * 8]
    sum_first(1, tiles_two)
    sum_second(1, tiles_two)
    sum_third(1, tiles_two)
    sum_end(1, tiles_two)
    wide = jnp.concatenate([sum_out[1][i] for i in range(tiles_two)], 0) * SCALE
    coupling = jnp.concatenate([wide[:, :NEW], wide[: PANEL - half, NEW:]], 0)
    square = wide[PANEL - half :, NEW:]
    coupling_ref[...] = coupling.T
    gram = square - tn(coupling, coupling)
    projected = basis[PANEL:] - tn(coupling, basis[:PANEL])
    upper_two, inverse_two = factor(gram)
    factor_second_ref[...] = upper_two
    lay_out(nn(inverse_two, projected), turn_second, second_ref)

    sum_sent(0, tiles_one)
    sum_sent(1, tiles_two)


def hand_over(*refs):
    n = len(refs) // 2
    copies = [pltpu.make_async_copy(refs[i], refs[n + i], refs[-1].at[i]) for i in range(n)]
    for copy in copies:
        copy.start()
    for copy in copies:
        copy.wait()


def per_device(start, stiff, convect, column_index, upwind):
    vmem = pl.BlockSpec(memory_space=pltpu.VMEM)
    hbm = pl.BlockSpec(memory_space=pl.ANY)
    f32 = jnp.float32
    rows = pltpu.VMEM((HALVES, OWN, 4, 128), f32)
    sums = lambda: [pltpu.VMEM((16, 8, 128), f32) for _ in range(2)]
    results = pl.pallas_call(
        kernel,
        out_shape=(
            jax.ShapeDtypeStruct((OWN, PANEL * BS), f32),
            jax.ShapeDtypeStruct((OWN, NEW * BS), f32),
            jax.ShapeDtypeStruct((PANEL, PANEL), f32),
            jax.ShapeDtypeStruct((NEW, PANEL), f32),
            jax.ShapeDtypeStruct((NEW, NEW), f32),
        ),
        in_specs=[vmem, hbm, hbm, hbm, hbm],
        out_specs=(vmem,) * 5,
        scratch_shapes=[
            [[pltpu.VMEM((GROUP, 4, 128), f32) for _ in range(HALVES)] for _ in range(POWERS)],
            rows,
            [rows for _ in range(POWERS)],
            [rows for _ in range(POWERS)],
            [[pltpu.VMEM((2, OWN, 4, 128), f32) for _ in range(HALVES)] for _ in range(POWERS)],
            pltpu.VMEM((OWN, BS, SLOTS * BS), f32),
            pltpu.VMEM((OWN, BS, BS), f32),
            pltpu.VMEM((OWN, 3 * BS, 8 * BS), jnp.bfloat16),
            pltpu.VMEM((OWN, 3 * BS, 2 * BS), jnp.bfloat16),
            pltpu.VMEM((OWN, PART, BS), f32),
            pltpu.VMEM((ALL, WIDE), f32),
            pltpu.VMEM((PANEL + NEW, WIDE), f32),
            pltpu.VMEM((RHS, PANEL), f32),
            pltpu.VMEM((PANEL + NEW, NEW), f32),
            pltpu.VMEM((PANEL, OWN, 2 * BS), f32),
            pltpu.VMEM((NEW, OWN, 2 * BS), f32),
            pltpu.VMEM((2, OWN, SLOTS), jnp.int32),
            pltpu.SMEM((OWN, SLOTS), jnp.int32),
            pltpu.SMEM((OWN, SLOTS), jnp.int32),
            pltpu.SMEM((OWN, SLOTS), jnp.int32),
            pltpu.SMEM((OWN, SLOTS), jnp.int32),
            sums(),
            sums(),
            sums(),
            sums(),
            pltpu.SemaphoreType.DMA((POWERS, HALVES)),
            pltpu.SemaphoreType.DMA((POWERS, HALVES)),
            pltpu.SemaphoreType.DMA((POWERS, HALVES, 2)),
            pltpu.SemaphoreType.DMA((POWERS, HALVES, 2)),
            pltpu.SemaphoreType.DMA((2,)),
            pltpu.SemaphoreType.DMA((2,)),
            pltpu.SemaphoreType.DMA((6,)),
            pltpu.SemaphoreType.DMA((2, 3)),
            pltpu.SemaphoreType.DMA((2, 3)),
        ],
        compiler_params=pltpu.CompilerParams(
            collective_id=0, has_side_effects=True, vmem_limit_bytes=56 << 20
        ),
    )(start, stiff, convect, column_index, upwind)
    first, second, factor_first, coupling, factor_second = pl.pallas_call(
        hand_over,
        out_shape=tuple(jax.ShapeDtypeStruct(x.shape, f32) for x in results),
        in_specs=[vmem] * len(results),
        out_specs=(hbm,) * len(results),
        scratch_shapes=[pltpu.SemaphoreType.DMA((len(results),))],
    )(*results)
    return first, second, factor_first, coupling.T, factor_second


def solution(mesh):
    return jax.shard_map(
        per_device,
        mesh=mesh,
        in_specs=(
            P(("row", "col"), None),
            P(("row", "col"), None, None),
            P(("row", "col"), None, None),
            P(("row", "col"), None),
            P(("row", "col"), None),
        ),
        out_specs=(P(("row", "col"), None), P(("row", "col"), None), P(), P(), P()),
        check_vma=False,
    )
```

```python
import functools

import jax
import jax.numpy as jnp
from jax import lax
from jax.experimental import pallas as pl
from jax.experimental.pallas import tpu as pltpu
from jax.sharding import PartitionSpec as P

MESH = pl.DeviceIdType.MESH
HIGHEST = lax.Precision.HIGHEST
STEPS = 4
POWERS = 2 * STEPS
BS = 64
RHS = 16
SLOTS = 9
OWN = 8
COLS = 16
SIDE = 4
ROWS_AXIS = 16
GROUP = OWN * COLS
PANEL = (STEPS + 1) * RHS
NEW = STEPS * RHS
ALL = (POWERS + 1) * RHS
WIDE = OWN * BS
HALVES = 2
PART = RHS // HALVES
SCALE = 1.0 / (GROUP * ROWS_AXIS * BS)


def dot(a, b, contract):
    return lax.dot_general(
        a, b, (contract, ((), ())), precision=HIGHEST, preferred_element_type=jnp.float32
    )


def nt(a, b):
    return dot(a, b, ((1,), (1,)))


def nn(a, b):
    return dot(a, b, ((1,), (0,)))


def tn(a, b):
    return dot(a, b, ((0,), (0,)))


def parts(x):
    high = x.astype(jnp.bfloat16).astype(jnp.float32)
    rest = x - high
    middle = rest.astype(jnp.bfloat16).astype(jnp.float32)
    return [high, middle, rest - middle]


def weight_parts(x):
    return jnp.concatenate(parts(x), 0).astype(jnp.bfloat16)


def product(near, weights):
    left = jnp.concatenate(parts(near) + [jnp.zeros_like(near)], 0).astype(jnp.bfloat16)
    every = lax.dot_general(left, weights, (((1,), (1,)), ((), ())), preferred_element_type=jnp.float32)
    total = every[16:24] + every[8:16] + every[:8]
    return total[:, 2 * BS :] + total[:, BS : 2 * BS] + total[:, :BS]


def local_row(index):
    return lax.bitwise_and(index, GROUP - 1)


def side_by_side(a, b):
    low = lax.broadcasted_iota(jnp.int32, a.shape, 1) < BS
    top = jnp.where(low, a, pltpu.roll(b, BS, 1))
    bottom = jnp.where(low, pltpu.roll(a, BS, 1), b)
    return jnp.concatenate([top, bottom], 0)


def factor(gram):
    n = gram.shape[0]
    tiles = n // 8
    shape = (8, n)
    sub = lax.broadcasted_iota(jnp.int32, shape, 0)
    lane = lax.broadcasted_iota(jnp.int32, shape, 1)
    left = [gram[8 * i : 8 * i + 8] for i in range(tiles)]
    right = [jnp.where(lane == sub + 8 * i, 1.0, 0.0) for i in range(tiles)]
    upper, inverse = [], []
    for k in range(tiles):
        columns = [
            [jnp.broadcast_to(left[i][:, 8 * k + j : 8 * k + j + 1], shape) if i >= k else None for i in range(tiles)]
            for j in range(8)
        ]
        pivots = jnp.ones(shape, jnp.float32)
        for j in range(8):
            pivot = columns[j][k][j : j + 1]
            scale = 1.0 / pivot
            pivots = jnp.where(sub == j, pivot, pivots)
            across = [columns[c][k][j : j + 1] for c in range(8)]
            row_left, row_right = left[k][j : j + 1], right[k][j : j + 1]
            for i in range(k, tiles):
                gain = columns[j][i] * scale
                if i == k:
                    gain = jnp.where(sub > j, gain, 0.0)
                for c in range(j + 1, 8):
                    columns[c][i] = columns[c][i] - gain * across[c]
                left[i] = left[i] - gain * row_left
                right[i] = right[i] - gain * row_right
        scale = lax.rsqrt(pivots)
        scale = scale * (1.5 - 0.5 * pivots * scale * scale)
        upper.append(jnp.where(lane >= sub + 8 * k, left[k], 0.0) * scale)
        inverse.append(right[k] * scale)
    return jnp.concatenate(upper, 0), jnp.concatenate(inverse, 0)


def kernel(
    start_ref, stiff_hbm, convect_hbm, index_hbm, upwind_hbm,
    first_ref, second_ref, factor_first_ref, coupling_ref, factor_second_ref,
    field, start_tiles, rows_twin, rows_far, give, stiff_ref, convect_ref, w_main, w_far, partial, powers, basis, mix_ref, both_ref, turn_first, turn_second, first_out,
    index_in, index_ref, upwind_ref, index_twin, index_far,
    sum_in, sum_a, sum_b, sum_out,
    send_sem, recv_sem, far_send, far_recv, index_send, index_recv, local_sem,
    sum_send, sum_recv,
):
    row = lax.axis_index("row")
    col = lax.axis_index("col")
    away = lambda i: min(i, SIDE - i)
    steps = sorted(
        ((i, j) for i in range(SIDE) for j in range(SIDE) if i or j), key=lambda p: -away(p[0]) - away(p[1])
    )
    sector_peers = [
        (row, lax.rem(col // SIDE + i, SIDE) * SIDE + lax.rem(lax.rem(col, SIDE) + j, SIDE)) for i, j in steps
    ]
    ring = sorted(range(1, ROWS_AXIS), key=lambda i: -min(i, ROWS_AXIS - i))
    row_peers = [(lax.rem(row + i, ROWS_AXIS), col) for i in ring]
    odd = lax.rem(row, 2)
    twin = (row + 1 - 2 * odd, col)
    far = (lax.rem(row + ROWS_AXIS - 1 + 2 * odd, ROWS_AXIS), col)
    slot_twin, slot_far = SLOTS - 2 + odd, SLOTS - 1 - odd

    barrier = pltpu.get_barrier_semaphore()
    for peer in sector_peers + [twin, far]:
        pl.semaphore_signal(barrier, inc=1, device_id=peer, device_id_type=MESH)
    loads = [
        pltpu.make_async_copy(src, dst, local_sem.at[i])
        for i, (src, dst) in enumerate(
            [(index_hbm, index_ref), (upwind_hbm, upwind_ref), (convect_hbm, convect_ref), (stiff_hbm, stiff_ref)]
        )
    ]
    for copy in loads:
        copy.start()
    own = pl.ds(col * OWN, OWN)
    for h in range(HALVES):
        for m in range(4):
            c = (h * PART + m) * BS
            start_tiles[h, :, m, :] = jnp.concatenate([start_ref[:, c : c + BS], start_ref[:, c + 4 * BS : c + 5 * BS]], 1)
        field[0][h][own] = start_tiles[h]
    pl.semaphore_wait(barrier, COLS + 1)

    pending = []

    def push(src, dst, send, recv, peer):
        copy = pltpu.make_async_remote_copy(
            src_ref=src, dst_ref=dst, send_sem=send, recv_sem=recv, device_id=peer, device_id_type=MESH
        )
        copy.start()
        return copy

    def arrived(ref, sem):
        pltpu.make_async_copy(ref, ref, sem).wait()

    def others(t, h):
        return field[t][h].at[pl.ds(0, GROUP - OWN)]

    def spread(t, h):
        mine = field[t][h].at[own]
        for peer in sector_peers:
            push(mine, mine, send_sem.at[t, h], recv_sem.at[t, h], peer)

    def keep(t, h, rows):
        for b in range(0, OWN, 2):
            powers[t * RHS + h * PART : t * RHS + (h + 1) * PART, b * BS : (b + 2) * BS] = rows(b)

    def sum_first(s, tiles):
        for peer in sector_peers:
            @pl.when(peer[1] < tiles)
            def _(peer=peer):
                push(sum_in[s].at[peer[1]], sum_a[s].at[col], sum_send.at[s, 0], sum_recv.at[s, 0], peer)

    def sum_second(s, tiles):
        @pl.when(col < tiles)
        def _():
            sum_a[s][col] = sum_in[s][col]
            arrived(sum_a[s].at[pl.ds(0, COLS - 1)], sum_recv.at[s, 0])
            sum_b[s][row] = total_of(sum_a[s])
            for peer in row_peers:
                push(sum_b[s].at[row], sum_b[s].at[row], sum_send.at[s, 1], sum_recv.at[s, 1], peer)

    def sum_third(s, tiles):
        @pl.when(col < tiles)
        def _():
            arrived(sum_b[s].at[pl.ds(0, ROWS_AXIS - 1)], sum_recv.at[s, 1])
            sum_out[s][col] = total_of(sum_b[s])
            for peer in sector_peers:
                push(sum_out[s].at[col], sum_out[s].at[col], sum_send.at[s, 2], sum_recv.at[s, 2], peer)

    def sum_end(s, tiles):
        @pl.when(col < tiles)
        def _():
            arrived(sum_out[s].at[pl.ds(0, tiles - 1)], sum_recv.at[s, 2])

        @pl.when(col >= tiles)
        def _():
            arrived(sum_out[s].at[pl.ds(0, tiles)], sum_recv.at[s, 2])

    def sum_sent(s, tiles):
        @pl.when(col < tiles)
        def _():
            arrived(sum_in[s].at[pl.ds(0, tiles - 1)], sum_send.at[s, 0])
            arrived(sum_b[s].at[pl.ds(0, ROWS_AXIS - 1)], sum_send.at[s, 1])
            arrived(sum_out[s].at[pl.ds(0, COLS - 1)], sum_send.at[s, 2])

        @pl.when(col >= tiles)
        def _():
            arrived(sum_in[s].at[pl.ds(0, tiles)], sum_send.at[s, 0])

    def total_of(ref):
        terms = [ref[i] for i in range(16)]
        while len(terms) > 1:
            terms = [terms[i] + terms[i + 1] for i in range(0, len(terms), 2)]
        return terms[0]

    for h in range(HALVES):
        spread(0, h)
    pending.append(push(index_hbm, index_in.at[0], index_send.at[0], index_recv.at[0], twin))
    pending.append(push(index_hbm, index_in.at[1], index_send.at[1], index_recv.at[1], far))
    for h in range(HALVES):
        keep(0, h, lambda b: side_by_side(start_tiles[h, b], start_tiles[h, b + 1]))

    for copy in loads:
        copy.wait()
    for b in range(OWN):
        flags = [upwind_ref[b, j].astype(jnp.float32) for j in range(SLOTS)]
        total = functools.reduce(lambda x, y: x + y, flags)
        flags[0] = flags[0] - total
        convect = convect_ref[b]
        blocks = [stiff_ref[b, :, j * BS : (j + 1) * BS] + flags[j] * convect for j in range(SLOTS)]
        blocks.insert(7, jnp.zeros_like(convect))
        w_main[b] = weight_parts(jnp.concatenate(blocks[:8], 1))
        near_far = [jnp.where(odd == 0, blocks[9], blocks[8]), jnp.where(odd == 0, blocks[8], blocks[9])]
        w_far[b] = weight_parts(jnp.concatenate(near_far, 1))

    arrived(index_in.at[0], index_recv.at[0])
    arrived(index_in.at[1], index_recv.at[1])
    local = [
        pltpu.make_async_copy(index_in.at[0], index_twin, local_sem.at[4]),
        pltpu.make_async_copy(index_in.at[1], index_far, local_sem.at[5]),
    ]
    for copy in local:
        copy.start()
    for copy in local:
        copy.wait()

    def apply(t, h, beside=()):
        f = field[t][h]
        arrived(others(t, h), recv_sem.at[t, h])
        for b in range(OWN):
            give[t][h][0, b] = f[local_row(index_far[b, slot_far])]
        pending.append(push(give[t][h].at[0], rows_far[t].at[h], far_send.at[t, h, 0], far_recv.at[t, h, 0], far))
        for b in range(OWN):
            give[t][h][1, b] = f[local_row(index_twin[b, slot_twin])]
        pending.append(push(give[t][h].at[1], rows_twin[t].at[h], far_send.at[t, h, 1], far_recv.at[t, h, 1], twin))
        for b in range(OWN):
            tiles = [f[col * OWN + b]] + [f[local_row(index_ref[b, j])] for j in range(1, 7)]
            tiles.append(jnp.zeros_like(tiles[0]))
            near = jnp.concatenate([side_by_side(tiles[j], tiles[j + 1]) for j in range(0, 8, 2)], 1)
            partial[b] = product(near, w_main[b])
        arrived(rows_twin[t].at[h], far_recv.at[t, h, 1])
        for call in beside:
            call()
        arrived(rows_far[t].at[h], far_recv.at[t, h, 0])
        results = []
        for b in range(OWN):
            near = side_by_side(rows_twin[t][h, b], rows_far[t][h, b])
            result = partial[b] + product(near, w_far[b])
            results.append(result)
        for b, result in enumerate(results):
            if t + 1 < POWERS:
                field[t + 1][h][col * OWN + b] = jnp.concatenate([result[:4], result[4:]], 1)
        if t + 1 < POWERS:
            spread(t + 1, h)
        keep(t + 1, h, lambda b: jnp.concatenate([results[b], results[b + 1]], 1))
        arrived(others(t, h), send_sem.at[t, h])
        for copy in pending:
            copy.wait_send()
        pending.clear()

    def gram_first():
        panel = powers[:PANEL, :]
        gram = nt(panel, panel)
        wide = jnp.concatenate([gram, jnp.zeros((PANEL, 128 - PANEL), jnp.float32)], 1)
        for i in range(tiles_one):
            sum_in[0][i] = wide[i * 8 : (i + 1) * 8]
        sum_first(0, tiles_one)

    def factor_one():
        sum_end(0, tiles_one)
        gram = jnp.concatenate([sum_out[0][i] for i in range(tiles_one)], 0)[:, :PANEL] * SCALE
        upper_one, inverse_one = factor(gram)
        factor_first_ref[...] = upper_one
        basis[:PANEL] = nn(inverse_one, powers[:PANEL, :])
        mix_ref[...] = inverse_one[PANEL - RHS :]

    def mix_early():
        for k in range(1, STEPS):
            basis[PANEL + (k - 1) * RHS : PANEL + k * RHS] = nn(mix_ref[...], powers[k * RHS : k * RHS + PANEL])
        both_ref[: PANEL + early, :early] = nt(basis[: PANEL + early], basis[PANEL : PANEL + early])

    def lay_out(value, turn, out_ref):
        n = value.shape[0]
        low = lax.broadcasted_iota(jnp.int32, (OWN, 2 * BS), 1) < BS
        for b in range(OWN):
            pair = value[:, b // 2 * 2 * BS : (b // 2 + 1) * 2 * BS]
            turn[:, b, :] = pair if b % 2 == 0 else pltpu.roll(pair, BS, 1)
        for p in range(0, n, 2):
            out_ref[:, p * BS : (p + 2) * BS] = jnp.where(low, turn[p], pltpu.roll(turn[p + 1], BS, 1))

    early = NEW - RHS
    tiles_one = PANEL // 8
    for t in range(STEPS):
        for h in range(HALVES):
            apply(t, h)
    gram_first()
    apply(4, 0)
    apply(4, 1)
    sum_second(0, tiles_one)
    apply(5, 0)
    apply(5, 1)
    sum_third(0, tiles_one)
    apply(6, 0)
    apply(6, 1)
    factor_one()
    apply(7, 0, [mix_early])
    leave = pltpu.make_async_copy(first_out, first_ref, local_sem.at[6])

    def first_leaves():
        lay_out(basis[:PANEL], turn_first, first_out)
        leave.start()

    apply(7, 1, [first_leaves])
    leave.wait()
    last = nn(mix_ref[...], powers[STEPS * RHS :])
    basis[PANEL + early :] = last
    both_ref[:, early:] = nt(basis[...], last)
    both_ref[PANEL + early :, :early] = nt(last, basis[PANEL : PANEL + early])

    both = both_ref[...]
    half = (PANEL + NEW) // 2
    tiles_two = half // 8
    wide = jnp.concatenate([both[:half], both[half:]], 1)
    for i in range(tiles_two):
        sum_in[1][i] = wide[i * 8 : (i + 1) * 8]
    sum_first(1, tiles_two)
    sum_second(1, tiles_two)
    sum_third(1, tiles_two)
    sum_end(1, tiles_two)
    wide = jnp.concatenate([sum_out[1][i] for i in range(tiles_two)], 0) * SCALE
    coupling = jnp.concatenate([wide[:, :NEW], wide[: PANEL - half, NEW:]], 0)
    square = wide[PANEL - half :, NEW:]
    coupling_ref[...] = coupling.T
    gram = square - tn(coupling, coupling)
    projected = basis[PANEL:] - tn(coupling, basis[:PANEL])
    upper_two, inverse_two = factor(gram)
    factor_second_ref[...] = upper_two
    lay_out(nn(inverse_two, projected), turn_second, second_ref)

    sum_sent(0, tiles_one)
    sum_sent(1, tiles_two)


def hand_over(*refs):
    n = len(refs) // 2
    copies = [pltpu.make_async_copy(refs[i], refs[n + i], refs[-1].at[i]) for i in range(n)]
    for copy in copies:
        copy.start()
    for copy in copies:
        copy.wait()


def per_device(start, stiff, convect, column_index, upwind):
    vmem = pl.BlockSpec(memory_space=pltpu.VMEM)
    hbm = pl.BlockSpec(memory_space=pl.ANY)
    f32 = jnp.float32
    rows = pltpu.VMEM((HALVES, OWN, 4, 128), f32)
    sums = lambda: [pltpu.VMEM((16, 8, 128), f32) for _ in range(2)]
    results = pl.pallas_call(
        kernel,
        out_shape=(
            jax.ShapeDtypeStruct((OWN, PANEL * BS), f32),
            jax.ShapeDtypeStruct((OWN, NEW * BS), f32),
            jax.ShapeDtypeStruct((PANEL, PANEL), f32),
            jax.ShapeDtypeStruct((NEW, PANEL), f32),
            jax.ShapeDtypeStruct((NEW, NEW), f32),
        ),
        in_specs=[vmem, hbm, hbm, hbm, hbm],
        out_specs=(hbm,) + (vmem,) * 4,
        scratch_shapes=[
            [[pltpu.VMEM((GROUP, 4, 128), f32) for _ in range(HALVES)] for _ in range(POWERS)],
            rows,
            [rows for _ in range(POWERS)],
            [rows for _ in range(POWERS)],
            [[pltpu.VMEM((2, OWN, 4, 128), f32) for _ in range(HALVES)] for _ in range(POWERS)],
            pltpu.VMEM((OWN, BS, SLOTS * BS), f32),
            pltpu.VMEM((OWN, BS, BS), f32),
            pltpu.VMEM((OWN, 3 * BS, 8 * BS), jnp.bfloat16),
            pltpu.VMEM((OWN, 3 * BS, 2 * BS), jnp.bfloat16),
            pltpu.VMEM((OWN, PART, BS), f32),
            pltpu.VMEM((ALL, WIDE), f32),
            pltpu.VMEM((PANEL + NEW, WIDE), f32),
            pltpu.VMEM((RHS, PANEL), f32),
            pltpu.VMEM((PANEL + NEW, NEW), f32),
            pltpu.VMEM((PANEL, OWN, 2 * BS), f32),
            pltpu.VMEM((NEW, OWN, 2 * BS), f32),
            pltpu.VMEM((OWN, PANEL * BS), f32),
            pltpu.VMEM((2, OWN, SLOTS), jnp.int32),
            pltpu.SMEM((OWN, SLOTS), jnp.int32),
            pltpu.SMEM((OWN, SLOTS), jnp.int32),
            pltpu.SMEM((OWN, SLOTS), jnp.int32),
            pltpu.SMEM((OWN, SLOTS), jnp.int32),
            sums(),
            sums(),
            sums(),
            sums(),
            pltpu.SemaphoreType.DMA((POWERS, HALVES)),
            pltpu.SemaphoreType.DMA((POWERS, HALVES)),
            pltpu.SemaphoreType.DMA((POWERS, HALVES, 2)),
            pltpu.SemaphoreType.DMA((POWERS, HALVES, 2)),
            pltpu.SemaphoreType.DMA((2,)),
            pltpu.SemaphoreType.DMA((2,)),
            pltpu.SemaphoreType.DMA((7,)),
            pltpu.SemaphoreType.DMA((2, 3)),
            pltpu.SemaphoreType.DMA((2, 3)),
        ],
        compiler_params=pltpu.CompilerParams(
            collective_id=0, has_side_effects=True, vmem_limit_bytes=56 << 20
        ),
    )(start, stiff, convect, column_index, upwind)
    first, second, factor_first, coupling, factor_second = pl.pallas_call(
        hand_over,
        out_shape=tuple(jax.ShapeDtypeStruct(x.shape, f32) for x in results),
        in_specs=[vmem] * len(results),
        out_specs=(hbm,) * len(results),
        scratch_shapes=[pltpu.SemaphoreType.DMA((len(results),))],
    )(*results)
    return first, second, factor_first, coupling.T, factor_second


def solution(mesh):
    return jax.shard_map(
        per_device,
        mesh=mesh,
        in_specs=(
            P(("row", "col"), None),
            P(("row", "col"), None, None),
            P(("row", "col"), None, None),
            P(("row", "col"), None),
            P(("row", "col"), None),
        ),
        out_specs=(P(("row", "col"), None), P(("row", "col"), None), P(), P(), P()),
        check_vma=False,
    )
```
